32 devices in a mesh: gx: 8 (over z, y), gy: 4 (over x, core).
Axes of the slice: x: 2, y: 2, z: 4, core: 2. Of those that a mesh axis runs over, the one named last changes fastest.
Arguments:
- field: float32 [32, 32, 64, 128], P(None, 'gx', 'gy'), may hold values from -6 to 6
- rates: float32 [32], replicated, may hold values from 0.2 to 1
- mixing: float32 [32, 32], replicated, may hold values from -1 to 1
- secretion: float32 [32, 8, 16, 256], P(None, 'gx', 'gy'), may hold values from -6 to 6
- positions: float32 [3, 8, 16, 256], P(None, 'gx', 'gy'), may hold values from 0 to 128, as said below
- stiffness: float32 [8, 16, 256], P('gx', 'gy'), may hold values from 0.5 to 2
- occupancy: int32 [8, 16, 256], P('gx', 'gy'), may hold values from 0 to 1
- offsets: int32 [8, 16, 256], P('gx', 'gy'), may hold values from 0 to 127
- migrant_state: float32 [8, 280, 512], P(None, 'gx', 'gy'), may hold values from -6 to 6
- migrant_live: int32 [8, 8, 512], P(None, 'gx', 'gy'), may hold values 0 or 1
Outputs:
- new_field: float32 [32, 32, 64, 128], P(None, 'gx', 'gy')
- displacement: float32 [3, 8, 16, 256], P(None, 'gx', 'gy')
- arrived: float32 [8, 280, 512], P(None, 'gx', 'gy')
The draws below stay inside these ranges and needn't reach their ends.
Inputs may be any that keep to these rules, and one draw needn't show every extreme that they name: `positions`: a slot's coordinates lie inside the box of its bin.
All inputs are finite; a program needn't handle non-finite values. No bound on the sum of `migrant_live` on one device may be relied on, other than what follows from the above.
Results may differ from the reference program's by a relative error of at most 0.0003.
Values sent between devices are 32-bit elements; how exact they have to be, the bound alone decides.
A program may use at most 64 MiB of HBM per device.

```python
import functools
import math
import jax
import jax.numpy as jnp
from jax import lax

S = 32
NZ = 128
BIN_XY = 4
BIN_Z = 8
SLOTS = 16
MIG = 128
SUBSTEPS = 4
BZ = 16
NX = 32
NY = 64
NBX = 8
NBY = 16
STATE = 35
N_GX = 8
N_GY = 4


def draw_positions(key, part):
    shape = (3, NBX, NBY, BZ * SLOTS)
    within = jax.random.uniform(key, shape, jnp.float32)
    plane = lax.broadcasted_iota(jnp.int32, shape, 0)
    bin_x = lax.broadcasted_iota(jnp.int32, shape, 1)
    bin_y = lax.broadcasted_iota(jnp.int32, shape, 2)
    bin_z = lax.broadcasted_iota(jnp.int32, shape, 3) // SLOTS
    start = jnp.where(plane == 0, bin_x * BIN_XY, jnp.where(plane == 1, bin_y * BIN_XY, bin_z * BIN_Z))
    extent = jnp.where(plane == 2, BIN_Z, BIN_XY)
    return (start.astype(jnp.float32) + within * extent.astype(jnp.float32) * 0.999).astype(jnp.float32)


def draw_occupancy(key, part):
    shape = (NBX, NBY, BZ * SLOTS)
    bin_x = lax.broadcasted_iota(jnp.int32, shape, 0)
    bin_y = lax.broadcasted_iota(jnp.int32, shape, 1)
    distant = jnp.abs(2 * bin_x + 1 - NBX) * 6 // NBX + jnp.abs(2 * bin_y + 1 - NBY) * 6 // NBY
    level = jnp.maximum(3, 15 - distant)
    rolled = jax.random.randint(key, shape, 0, 16)
    return (rolled < level).astype(jnp.int32)


def plant(values, stream_key, low, top_value):
    shape = values.shape
    place = [jax.random.randint(jax.random.fold_in(stream_key, axis), (), 0, shape[axis]) for axis in range(len(shape))]
    values = values.at[tuple(place)].set(low)
    longest = shape.index(max(shape))
    place[longest] = (place[longest] + 1) % shape[longest]
    return values.at[tuple(place)].set(top_value)


def block_scale(stream_key, dims, shards, smallest, top_value):
    level = 1.0
    for position, blocks in shards:
        heights = jax.random.uniform(jax.random.fold_in(jax.random.fold_in(stream_key, 6), position), (blocks,), jnp.float32, smallest / len(shards), top_value / len(shards))
        level = level * jnp.repeat(jnp.exp(heights), dims[position] // blocks).reshape((-1,) + (1,) * (len(dims) - 1 - position))
    return level


def centred(own_key, shape, spread, most, shards=(), kind=jnp.bfloat16):
    result = jax.random.normal(own_key, shape, jnp.float32) * spread
    if len(shards) > 0:
        result = block_scale(own_key, shape, shards, -0.22, 0.18) * result
    return jnp.clip(result, min=-most, max=most).astype(kind)


def setup_inputs(seed: int = 0) -> dict:
    streams_of = jax.random.split(jax.random.key(seed), 11)
    field = centred(streams_of[0], (S, NX, NY, NZ), 1.0, 6.0, ((1, 8), (2, 4)), jnp.float32)
    rates = jnp.clip(jnp.exp(jax.random.uniform(streams_of[1], (S,), jnp.float32, math.log(0.2), math.log(1.0))), 0.2, 1.0)
    mixing = centred(streams_of[2], (S, S), S ** -0.5, 1.0, (), jnp.float32)
    secretion = centred(streams_of[3], (S, NBX, NBY, BZ * SLOTS), 1.0, 6.0, ((1, 8), (2, 4)), jnp.float32)
    positions = draw_positions(jax.random.fold_in(streams_of[10], 71), 0)
    stiffness = jnp.clip(jnp.exp(math.log(2.0) - 1.3862944 * jax.random.uniform(streams_of[5], (NBX, NBY, BZ * SLOTS), jnp.float32) ** block_scale(streams_of[5], (NBX, NBY, BZ * SLOTS), ((0, 8), (1, 4)), -0.2, 0.2)), 0.5, 2.0)
    occupancy = draw_occupancy(jax.random.fold_in(streams_of[10], 71), 0)
    offsets = plant(jax.random.randint(streams_of[7], (NBX, NBY, BZ * SLOTS), 0, BIN_XY * BIN_XY * BIN_Z), jax.random.fold_in(streams_of[7], 1), 0, (BIN_XY * BIN_XY * BIN_Z) - 1).astype(jnp.int32)
    migrant_state = centred(streams_of[8], (8, STATE * N_GX, MIG * N_GY), 1.0, 6.0, ((1, 8), (2, 4)), jnp.float32)
    migrant_live = plant((jax.random.randint(streams_of[9], (8, N_GX, MIG * N_GY), 0, 2) < 1).astype(jnp.int32), jax.random.fold_in(streams_of[9], 1), 0, 1)
    return {"field": field, "rates": rates, "mixing": mixing, "secretion": secretion, "positions": positions, "stiffness": stiffness, "occupancy": occupancy, "offsets": offsets, "migrant_state": migrant_state, "migrant_live": migrant_live}


time_step = 0.15
move_step = 0.1
spread_sq = 8.0
shifts = ((-1, -1), (-1, 0), (-1, 1), (0, -1), (0, 1), (1, -1), (1, 0), (1, 1))


def advance(padded, source, rates, mixing):
    center = padded[:, 1:-1, 1:-1, :]
    deeper = jnp.pad(center, ((0, 0), (0, 0), (0, 0), (1, 1)))
    beside = padded[:, 2:, 1:-1, :] + padded[:, :-2, 1:-1, :]
    beside = beside + padded[:, 1:-1, 2:, :] + padded[:, 1:-1, :-2, :]
    beside = beside + deeper[:, :, :, 2:] + deeper[:, :, :, :-2]
    laplace = beside - 6.0 * center
    species = center.shape[0]
    mixed = jnp.dot(mixing, center.reshape(species, -1), precision=lax.Precision.HIGHEST).reshape(center.shape)
    return center + time_step * (rates[:, None, None, None] * laplace) + time_step * mixed + time_step * source


def deposit(secretion, occupancy, offsets):
    species, bins_x, bins_y, lanes = secretion.shape
    shape = (bins_x, bins_y, lanes)
    cells_x = bins_x * BIN_XY
    cells_y = bins_y * BIN_XY
    cells_z = (lanes // SLOTS) * BIN_Z
    bin_x = lax.broadcasted_iota(jnp.int32, shape, 0)
    bin_y = lax.broadcasted_iota(jnp.int32, shape, 1)
    bin_z = lax.broadcasted_iota(jnp.int32, shape, 2) // SLOTS
    voxel_x = bin_x * BIN_XY + offsets // (BIN_XY * BIN_Z)
    voxel_y = bin_y * BIN_XY + (offsets // BIN_Z) % BIN_XY
    voxel_z = bin_z * BIN_Z + offsets % BIN_Z
    flat = ((voxel_x * cells_y + voxel_y) * cells_z + voxel_z).reshape(-1).astype(jnp.int32)
    values = (secretion * occupancy.astype(jnp.float32)[None]).reshape(species, -1)
    total = jnp.zeros((species, cells_x * cells_y * cells_z), jnp.float32).at[:, flat].add(values)
    return total.reshape(species, cells_x, cells_y, cells_z)


def pair_forces(points, padded, occupancy):
    planes, bins_x, bins_y, lanes = points.shape
    layers = lanes // SLOTS
    boxed = padded.reshape(planes, bins_x + 2, bins_y + 2, layers, SLOTS)
    boxed = jnp.pad(boxed, ((0, 0), (0, 0), (0, 0), (1, 1), (0, 0)))
    owned = points.reshape(planes, bins_x, bins_y, layers, SLOTS)[:3, :, :, :, :, None]
    force = jnp.zeros((3, bins_x, bins_y, layers, SLOTS), jnp.float32)
    for offset_x in range(3):
        nearby = jnp.concatenate([boxed[:, offset_x:offset_x + bins_x, offset_y:offset_y + bins_y, offset_z:offset_z + layers, :] for offset_y in range(3) for offset_z in range(3)], axis=-1)
        apart = owned - nearby[:3, :, :, :, None, :]
        strength = nearby[3][:, :, :, None, :] * jnp.exp(-jnp.sum(apart * apart, axis=0) / spread_sq)
        force = force + jnp.sum(apart * strength[None], axis=-1)
    active = occupancy.reshape(1, bins_x, bins_y, layers, SLOTS).astype(jnp.float32)
    return (move_step * active * force).reshape(3, bins_x, bins_y, lanes)


def row_forces(points, padded, occupancy, row_index):
    return pair_forces(lax.dynamic_slice_in_dim(points, row_index, 1, 1), lax.dynamic_slice_in_dim(padded, row_index, 3, 1), lax.dynamic_slice_in_dim(occupancy, row_index, 1, 0))


def reference(field, rates, mixing, secretion, positions, stiffness, occupancy, offsets, migrant_state, migrant_live):
    source = deposit(secretion, occupancy, offsets)
    current = field
    for substep in range(SUBSTEPS):
        padded = jnp.pad(current, ((0, 0), (1, 1), (1, 1), (0, 0)))
        current = advance(padded, source, rates, mixing)
    weight = stiffness * occupancy.astype(jnp.float32)
    points = jnp.concatenate([positions, weight[None]], axis=0)
    bordered = jnp.pad(points, ((0, 0), (1, 1), (1, 1), (0, 0)))
    rowwise = lax.map(functools.partial(row_forces, points, bordered, occupancy), jnp.arange(NBX, dtype=jnp.int32))
    displacement = jnp.moveaxis(rowwise[:, :, 0], 0, 1)
    payload = migrant_state.reshape(8, N_GX, STATE, N_GY, MIG) * migrant_live.reshape(8, N_GX, 1, N_GY, MIG).astype(jnp.float32)
    framed = jnp.pad(payload, ((0, 0), (1, 1), (0, 0), (1, 1), (0, 0)))
    pieces = []
    for index in range(8):
        move_x, move_y = shifts[index]
        pieces.append(framed[index, 1 - move_x:1 - move_x + N_GX, :, 1 - move_y:1 - move_y + N_GY, :])
    arrived = jnp.stack(pieces).reshape(migrant_state.shape)
    return current, displacement, arrived
```

```python
import jax
import jax.numpy as jnp
from jax import lax
from jax.experimental import pallas as pl
from jax.experimental.pallas import tpu as pltpu
from jax.sharding import PartitionSpec as P

BIN_XY = 4
BIN_Z = 8
SLOTS = 16
SUBSTEPS = 4
CHUNK = 8
GROUPS = 9

time_step = 0.15
move_step = 0.1
spread_sq = 8.0
shifts = ((-1, -1), (-1, 0), (-1, 1), (0, -1), (0, 1), (1, -1), (1, 0), (1, 1))
MESH = pl.DeviceIdType.MESH


def split(value):
    high = value.astype(jnp.bfloat16)
    return high, (value - high.astype(jnp.float32)).astype(jnp.bfloat16)


def kernel(
    field_ref, rates_ref, mixing_ref, sec_ref, pos_ref, stiff_ref, occ_ref, off_ref, state_ref, live_ref,
    out_ref, disp_ref, arrived_ref,
    buf, halo_x, halo_y, src, pts, nb, own, acc, payload,
    sx, rx, sy, ry, sp, rp, sm, rm, local,
):
    nx, ny, species, nz = buf.shape[1:]
    bins_y, lanes = stiff_ref.shape[1:]
    halves = ny // CHUNK
    gx, gy = lax.axis_index("gx"), lax.axis_index("gy")
    n_gx, n_gy = lax.axis_size("gx"), lax.axis_size("gy")

    def exists(dx, dy):
        ok = None
        for coord, count, delta in ((gx, n_gx, dx), (gy, n_gy, dy)):
            if delta != 0:
                one = coord > 0 if delta < 0 else coord < count - 1
                ok = one if ok is None else jnp.logical_and(ok, one)
        return ok

    def whither(dx, dy):
        return (gx + dx, gy + dy)

    load = pltpu.make_async_copy(field_ref, buf.at[0], local.at[0])
    load.start()

    barrier = pltpu.get_barrier_semaphore()
    for dx, dy in shifts:
        @pl.when(exists(dx, dy))
        def _(dx=dx, dy=dy):
            pl.semaphore_signal(barrier, inc=1, device_id=whither(dx, dy), device_id_type=MESH)

    weight = stiff_ref[0] * occ_ref[0].astype(jnp.float32)
    for by in range(bins_y):
        for plane in range(3):
            pts[1, by + 1, plane : plane + 1, :] = pos_ref[plane, 0, by : by + 1, :]
        pts[1, by + 1, 3:4, :] = weight[by : by + 1]
    for index in range(8):
        payload[index] = state_ref[index] * live_ref[index].astype(jnp.float32)

    across = 1 + (gx > 0).astype(jnp.int32) + (gx < n_gx - 1).astype(jnp.int32)
    along = 1 + (gy > 0).astype(jnp.int32) + (gy < n_gy - 1).astype(jnp.int32)
    pl.semaphore_wait(barrier, across * along - 1)
    load.wait()

    sides = (-1, 1)

    def face_x(t, side, half):
        rows = pl.ds(half * CHUNK, CHUNK)
        return pltpu.make_async_remote_copy(
            src_ref=buf.at[t, 0 if side == 0 else nx - 1, rows],
            dst_ref=halo_x.at[t, 1 - side, rows],
            send_sem=sx.at[t, side, half],
            recv_sem=rx.at[t, side, half],
            device_id=whither(sides[side], 0),
            device_id_type=MESH,
        )

    def face_y(t, side):
        return pltpu.make_async_remote_copy(
            src_ref=buf.at[t, :, 0 if side == 0 else ny - 1],
            dst_ref=halo_y.at[t, 1 - side],
            send_sem=sy.at[t, side],
            recv_sem=ry.at[t, side],
            device_id=whither(0, sides[side]),
            device_id_type=MESH,
        )

    def agents(index):
        dx, dy = shifts[index]
        if dy == 0:
            mine, theirs = pl.ds(1, bins_y), pl.ds(1, bins_y)
        elif dy > 0:
            mine, theirs = pl.ds(bins_y, 1), pl.ds(0, 1)
        else:
            mine, theirs = pl.ds(1, 1), pl.ds(bins_y + 1, 1)
        return pltpu.make_async_remote_copy(
            src_ref=pts.at[1, mine],
            dst_ref=pts.at[1 - dx, theirs],
            send_sem=sp.at[index],
            recv_sem=rp.at[index],
            device_id=whither(dx, dy),
            device_id_type=MESH,
        )

    def migrants(index):
        dx, dy = shifts[index]
        return pltpu.make_async_remote_copy(
            src_ref=payload.at[index],
            dst_ref=arrived_ref.at[index],
            send_sem=sm.at[index],
            recv_sem=rm.at[index],
            device_id=whither(dx, dy),
            device_id_type=MESH,
        )

    def send(copy, dx, dy):
        @pl.when(exists(dx, dy))
        def _():
            copy.start()

    def landed(copy, dx, dy):
        @pl.when(exists(-dx, -dy))
        def _():
            copy.wait_recv()

    for half in range(halves):
        for side in range(2):
            send(face_x(0, side, half), sides[side], 0)
        if half == 0:
            for side in range(2):
                send(face_y(0, side), 0, sides[side])
    for index in range(8):
        send(agents(index), *shifts[index])
    for index in range(8):
        send(migrants(index), *shifts[index])

    for side in range(2):
        @pl.when(jnp.logical_not(exists(sides[side], 0)))
        def _(side=side):
            def fill(row, carry):
                for t in range(SUBSTEPS):
                    halo_x[t, side, row] = jnp.zeros((species, nz), jnp.float32)
                return carry
            lax.fori_loop(0, ny, fill, 0)

        @pl.when(jnp.logical_not(exists(0, sides[side])))
        def _(side=side):
            for t in range(SUBSTEPS):
                halo_y[t, side] = jnp.zeros((nx, species, nz), jnp.float32)

    for index in range(8):
        dx, dy = shifts[index]

        @pl.when(jnp.logical_not(exists(-dx, -dy)))
        def _(index=index, dx=dx, dy=dy):
            arrived_ref[index] = jnp.zeros(arrived_ref.shape[1:], jnp.float32)
            rows = pl.ds(1, bins_y) if dy == 0 else pl.ds(0 if dy > 0 else bins_y + 1, 1)
            count = bins_y if dy == 0 else 1
            pts[1 - dx, rows] = jnp.zeros((count,) + pts.shape[2:], jnp.float32)

    depth = lax.broadcasted_iota(jnp.int32, (nz, lanes), 0)
    layer = lax.broadcasted_iota(jnp.int32, (1, lanes), 1) // SLOTS
    for by in range(bins_y):
        place = off_ref[0, by : by + 1, :]
        alive = occ_ref[0, by : by + 1, :].astype(jnp.float32) * time_step
        secreted = jnp.concatenate(split(sec_ref[:, 0, by, :] * alive), axis=0)
        cell = jnp.where(depth == layer * BIN_Z + (place & (BIN_Z - 1)), place >> 3, -1)

        def deposit(ox, carry, by=by, secreted=secreted, cell=cell):
            hits = jnp.concatenate(
                [
                    jnp.where(cell == ox * BIN_XY + oy, 1.0, 0.0).astype(jnp.bfloat16)
                    for oy in range(BIN_XY)
                ],
                axis=0,
            )
            total = lax.dot_general(
                secreted, hits, (((1,), (1,)), ((), ())), preferred_element_type=jnp.float32
            )
            total = total[:species] + total[species:]
            for oy in range(BIN_XY):
                src[ox, by * BIN_XY + oy] = total[:, oy * nz : (oy + 1) * nz]
            return carry

        lax.fori_loop(0, BIN_XY, deposit, 0)

    mix_high, mix_low = split(mixing_ref[...] * time_step)
    mix = jnp.concatenate([mix_high, mix_high, mix_low], axis=1)
    reach = rates_ref[...] * time_step
    keep = 1.0 - 6.0 * reach
    reach = jnp.broadcast_to(reach, (species, nz))
    keep = jnp.broadcast_to(keep, (species, nz))
    column = lax.broadcasted_iota(jnp.int32, (species, nz), 1)

    def block(t, x, half):
        first = half * CHUNK
        cells = jnp.concatenate([buf[t, x, first + k] for k in range(CHUNK)], axis=1)
        high, low = split(cells)
        mixed = jnp.dot(
            mix, jnp.concatenate([high, low, high], axis=0), preferred_element_type=jnp.float32
        )
        for k in range(CHUNK):
            y = first + k
            here = buf[t, x, y]
            beside = halo_x[t, 0, y] if x == 0 else buf[t, x - 1, y]
            beside = beside + (halo_x[t, 1, y] if x == nx - 1 else buf[t, x + 1, y])
            beside = beside + (halo_y[t, 0, x] if y == 0 else buf[t, x, y - 1])
            beside = beside + (halo_y[t, 1, x] if y == ny - 1 else buf[t, x, y + 1])
            beside = beside + jnp.where(column == 0, 0.0, pltpu.roll(here, 1, 1))
            beside = beside + jnp.where(column == nz - 1, 0.0, pltpu.roll(here, nz - 1, 1))
            buf[t + 1, x, y] = (
                keep * here + reach * beside + mixed[:, k * nz : (k + 1) * nz] + src[x, y]
            )

    def gather_agents():
        for index in range(8):
            landed(agents(index), *shifts[index])
        for group in range(GROUPS):
            dx, dy = group // 3, group % 3
            for by in range(bins_y):
                row = group * bins_y + by
                for plane in range(4):
                    nb[plane, row : row + 1, :] = pts[dx, by + dy, plane : plane + 1, :]
                for plane in range(3):
                    own[plane, row : row + 1, :] = pts[1, by + 1, plane : plane + 1, :]
        used = GROUPS * bins_y
        if nb.shape[1] > used:
            for plane in range(4):
                nb[plane, used:, :] = jnp.zeros((nb.shape[1] - used, lanes), jnp.float32)
            for plane in range(3):
                own[plane, used:, :] = jnp.zeros((nb.shape[1] - used, lanes), jnp.float32)
        acc[...] = jnp.zeros(acc.shape, jnp.float32)

    slot = lax.broadcasted_iota(jnp.int32, (1, lanes), 1)
    span = 2 * SLOTS - 1
    share = -(-(2 * span + 1) // (SUBSTEPS - 1))

    def forces(t):
        def pairs(k, carry):
            d = (t - 1) * share + k - span
            other = slot + d
            near = jnp.abs((other >> 4) - (slot >> 4)) <= 1
            near = jnp.logical_and(near, jnp.logical_and(other >= 0, other < lanes))
            turn = lax.rem(lanes - d, lanes)
            apart = [own[plane] - pltpu.roll(nb[plane], turn, 1) for plane in range(3)]
            heavy = jnp.where(near, pltpu.roll(nb[3], turn, 1), 0.0)
            square = apart[0] * apart[0] + apart[1] * apart[1] + apart[2] * apart[2]
            strength = heavy * jnp.exp(square * (-1.0 / spread_sq))
            for plane in range(3):
                acc[plane] += apart[plane] * strength
            return carry

        lax.fori_loop(0, share, pairs, 0)

    def substep(t, carry):
        for side in range(2):
            landed(face_y(t, side), 0, sides[side])
        for half in range(halves):
            for side in (1, 0):
                landed(face_x(t, side, half), sides[side], 0)
                mine = 1 - side
                block(t, 0 if mine == 0 else nx - 1, half)

                @pl.when(t < SUBSTEPS - 1)
                def _(mine=mine, half=half):
                    send(face_x(t + 1, mine, half), sides[mine], 0)

            if half == 0:
                for x in range(1, nx - 1):
                    for part in range(halves):
                        block(t, x, part)

                @pl.when(t == 1)
                def _():
                    gather_agents()

                @pl.when(t >= 1)
                def _():
                    forces(t)

        @pl.when(t < SUBSTEPS - 1)
        def _():
            for side in range(2):
                send(face_y(t + 1, side), 0, sides[side])

        return carry

    lax.fori_loop(0, SUBSTEPS, substep, 0)

    store = pltpu.make_async_copy(buf.at[SUBSTEPS], out_ref, local.at[0])
    store.start()
    scale = move_step * occ_ref[0].astype(jnp.float32)
    for plane in range(3):
        force = acc[plane, 0:bins_y, :]
        for group in range(1, GROUPS):
            force = force + acc[plane, group * bins_y : (group + 1) * bins_y, :]
        disp_ref[plane, 0] = scale * force

    for index in range(8):
        landed(migrants(index), *shifts[index])

    def sent(copy, dx, dy):
        @pl.when(exists(dx, dy))
        def _():
            copy.wait_send()

    for index in range(8):
        sent(agents(index), *shifts[index])
        sent(migrants(index), *shifts[index])

    def drain(t, carry):
        for side in range(2):
            for half in range(halves):
                sent(face_x(t, side, half), sides[side], 0)
            sent(face_y(t, side), 0, sides[side])
        return carry

    lax.fori_loop(0, SUBSTEPS, drain, 0)
    store.wait()


def on_device(
    field, rates, mixing, secretion, positions, stiffness, occupancy, offsets, migrant_state, migrant_live
):
    species, nx, ny, nz = field.shape
    bins_y, lanes = stiffness.shape[1:]
    halves = ny // CHUNK
    kinds, state, slots = migrant_state.shape
    rows = -(-GROUPS * bins_y // 8) * 8
    cells = jnp.transpose(field, (1, 2, 0, 3))
    vmem = pl.BlockSpec(memory_space=pltpu.VMEM)
    anywhere = pl.BlockSpec(memory_space=pl.ANY)
    dma = pltpu.SemaphoreType.DMA
    result, moved, arrived = pl.pallas_call(
        kernel,
        out_shape=(
            jax.ShapeDtypeStruct(cells.shape, jnp.float32),
            jax.ShapeDtypeStruct(positions.shape, jnp.float32),
            jax.ShapeDtypeStruct(migrant_state.shape, jnp.float32),
        ),
        in_specs=[anywhere] + [vmem] * 9,
        out_specs=(anywhere, vmem, vmem),
        scratch_shapes=[
            pltpu.VMEM((SUBSTEPS + 1, nx, ny, species, nz), jnp.float32),
            pltpu.VMEM((SUBSTEPS, 2, ny, species, nz), jnp.float32),
            pltpu.VMEM((SUBSTEPS, 2, nx, species, nz), jnp.float32),
            pltpu.VMEM((nx, ny, species, nz), jnp.float32),
            pltpu.VMEM((3, bins_y + 2, 8, lanes), jnp.float32),
            pltpu.VMEM((4, rows, lanes), jnp.float32),
            pltpu.VMEM((3, rows, lanes), jnp.float32),
            pltpu.VMEM((3, rows, lanes), jnp.float32),
            pltpu.VMEM(migrant_state.shape, jnp.float32),
            dma((SUBSTEPS, 2, halves)),
            dma((SUBSTEPS, 2, halves)),
            dma((SUBSTEPS, 2)),
            dma((SUBSTEPS, 2)),
            dma((8,)),
            dma((8,)),
            dma((8,)),
            dma((8,)),
            dma((1,)),
        ],
        compiler_params=pltpu.CompilerParams(
            collective_id=0, has_side_effects=True, vmem_limit_bytes=40 * 1024 * 1024
        ),
        name="tumour_step",
    )(
        cells,
        rates[:, None],
        mixing,
        secretion,
        positions,
        stiffness,
        occupancy,
        offsets,
        migrant_state,
        migrant_live,
    )
    return jnp.transpose(result, (2, 0, 1, 3)), moved, arrived


def solution(mesh):
    return jax.shard_map(
        on_device,
        mesh=mesh,
        in_specs=(
            P(None, "gx", "gy", None),
            P(),
            P(),
            P(None, "gx", "gy", None),
            P(None, "gx", "gy", None),
            P("gx", "gy", None),
            P("gx", "gy", None),
            P("gx", "gy", None),
            P(None, "gx", "gy"),
            P(None, "gx", "gy"),
        ),
        out_specs=(P(None, "gx", "gy", None), P(None, "gx", "gy", None), P(None, "gx", "gy")),
        check_vma=False,
    )
```

```python
import jax
import jax.numpy as jnp
from jax import lax
from jax.experimental import pallas as pl
from jax.experimental.pallas import tpu as pltpu
from jax.sharding import PartitionSpec as P

BIN_XY = 4
BIN_Z = 8
SLOTS = 16
SUBSTEPS = 4
CHUNK = 8
GROUPS = 9

time_step = 0.15
move_step = 0.1
spread_sq = 8.0
shifts = ((-1, -1), (-1, 0), (-1, 1), (0, -1), (0, 1), (1, -1), (1, 0), (1, 1))
MESH = pl.DeviceIdType.MESH


def split(value):
    high = value.astype(jnp.bfloat16)
    return high, (value - high.astype(jnp.float32)).astype(jnp.bfloat16)


def kernel(
    field_ref, rates_ref, mixing_ref, sec_ref, pos_ref, stiff_ref, occ_ref, off_ref, state_ref, live_ref,
    out_ref, disp_ref, arrived_ref,
    home, buf, swap_to, swap_from, face_to, face_from, edge_from, ends_to, ends_from,
    sec_to, sec_from, off_from, src, pts, nb, own, acc, payload, landing,
    s_swap, r_swap, s_face, r_face, s_edge, r_edge, s_ends, r_ends, s_sec, r_sec,
    s_pts, r_pts, s_mig, r_mig, local, stored,
):
    nx, ny, species, nz = home.shape
    bins_y, lanes = stiff_ref.shape[1:]
    halves = ny // CHUNK
    pairs = CHUNK // 2
    mid = nz // 2
    groups = ((0, nx - 1), tuple(range(1, nx - 1)))
    gx, gy = lax.axis_index("gx"), lax.axis_index("gy")
    n_gx, n_gy = lax.axis_size("gx"), lax.axis_size("gy")
    p = lax.rem(gx, 2)
    mate = (gx + 1 - 2 * p, gy)
    sides = (-1, 1)

    def exists(dx, dy):
        ok = None
        for coord, count, delta in ((gx, n_gx, dx), (gy, n_gy, dy)):
            if delta != 0:
                one = coord >= -delta if delta < 0 else coord < count - delta
                ok = one if ok is None else jnp.logical_and(ok, one)
        return ok

    load = pltpu.make_async_copy(field_ref, home, local.at[0])
    load.start()

    barrier = pltpu.get_barrier_semaphore()
    for dx, dy in shifts + ((-2, 0), (2, 0)):
        @pl.when(exists(dx, dy))
        def _(dx=dx, dy=dy):
            pl.semaphore_signal(barrier, inc=1, device_id=(gx + dx, gy + dy), device_id_type=MESH)

    alive = occ_ref[0].astype(jnp.float32)
    weight = stiff_ref[0] * alive
    for by in range(bins_y):
        for plane in range(3):
            pts[1, by + 1, plane : plane + 1, :] = pos_ref[plane, 0, by : by + 1, :]
        pts[1, by + 1, 3:4, :] = weight[by : by + 1]
        sec_to[by] = sec_ref[:, 0, by, :] * (alive[by : by + 1] * time_step)

    column = lax.broadcasted_iota(jnp.int32, (species, nz), 1)
    kept = (column // mid) == p
    low = column < mid
    inner = column & (mid - 1)
    rim = (1 - p) * (mid - 1)

    def turned(value):
        return pltpu.roll(value, mid, 1)

    def remote(src_ref, dst_ref, send_sem, recv_sem, device):
        return pltpu.make_async_remote_copy(
            src_ref=src_ref,
            dst_ref=dst_ref,
            send_sem=send_sem,
            recv_sem=recv_sem,
            device_id=device,
            device_id_type=MESH,
        )

    def swap(way, x, half):
        rows = pl.ds(half * pairs, pairs)
        return remote(
            swap_to.at[way, x, rows], swap_from.at[way, x, rows],
            s_swap.at[way, x, half], r_swap.at[way, x, half], mate,
        )

    def face(t, side, half):
        rows = pl.ds(half * pairs, pairs)
        return remote(
            face_to.at[t, side, rows], face_from.at[t, 1 - side, rows],
            s_face.at[t, side, half], r_face.at[t, side, half], (gx + 2 * sides[side], gy),
        )

    def edge(t, side, x):
        return remote(
            buf.at[t, x, 0 if side == 0 else ny - 1], edge_from.at[t, 1 - side, x],
            s_edge.at[t, side, x], r_edge.at[t, side, x], (gx, gy + sides[side]),
        )

    def ends(t, group):
        return remote(
            ends_to.at[t, group], ends_from.at[t, group],
            s_ends.at[t, group], r_ends.at[t, group], mate,
        )

    def secreted():
        width = lanes // 2
        return remote(
            sec_to.at[:, :, pl.ds(pl.multiple_of((1 - p) * width, width), width)],
            sec_from.at[:, :, pl.ds(pl.multiple_of(p * width, width), width)],
            s_sec.at[0], r_sec.at[0], mate,
        )

    def placed():
        return remote(off_ref, off_from, s_sec.at[1], r_sec.at[1], mate)

    def agents(index):
        dx, dy = shifts[index]
        if dy == 0:
            mine, theirs = pl.ds(1, bins_y), pl.ds(1, bins_y)
        elif dy > 0:
            mine, theirs = pl.ds(bins_y, 1), pl.ds(0, 1)
        else:
            mine, theirs = pl.ds(1, 1), pl.ds(bins_y + 1, 1)
        return remote(
            pts.at[1, mine], pts.at[1 - dx, theirs],
            s_pts.at[index], r_pts.at[index], (gx + dx, gy + dy),
        )

    def migrants(index):
        dx, dy = shifts[index]
        return remote(
            payload.at[index], landing.at[index],
            s_mig.at[index], r_mig.at[index], (gx + dx, gy + dy),
        )

    def send(copy, dx, dy):
        @pl.when(exists(dx, dy))
        def _():
            copy.start()

    def landed(copy, dx, dy):
        @pl.when(exists(-dx, -dy))
        def _():
            copy.wait_recv()

    def sent(copy, dx, dy):
        @pl.when(exists(dx, dy))
        def _():
            copy.wait_send()

    def leave(way, x, half, cells):
        for j in range(half * pairs, (half + 1) * pairs):
            swap_to[way, x, j] = jnp.where(kept, turned(cells(2 * j)), cells(2 * j + 1))
        swap(way, x, half).start()

    def enter(way, x, half, cells, keep_in):
        swap(way, x, half).wait_recv()
        for j in range(half * pairs, (half + 1) * pairs):
            came = swap_from[way, x, j]
            keep_in(2 * j, jnp.where(kept, cells(2 * j), came))
            keep_in(2 * j + 1, jnp.where(kept, cells(2 * j + 1), turned(came)))

    across = 1 + (gx > 0).astype(jnp.int32) + (gx < n_gx - 1).astype(jnp.int32)
    along = 1 + (gy > 0).astype(jnp.int32) + (gy < n_gy - 1).astype(jnp.int32)
    beyond = (gx > 1).astype(jnp.int32) + (gx < n_gx - 2).astype(jnp.int32)
    pl.semaphore_wait(barrier, across * along - 1 + beyond)

    secreted().start()
    placed().start()
    load.wait()
    order = [(x, half) for group in groups for half in range(halves) for x in group]
    for x, half in order:
        leave(0, x, half, lambda y, x=x: home[x, y])
    for index in range(8):
        send(agents(index), *shifts[index])
    for index in range(8):
        payload[index] = state_ref[:, index, :] * live_ref[index].astype(jnp.float32)
        send(migrants(index), *shifts[index])

    for side in range(2):
        @pl.when(jnp.logical_not(exists(2 * sides[side], 0)))
        def _(side=side):
            def fill(row, carry):
                for t in range(SUBSTEPS):
                    face_from[t, side, row] = jnp.zeros((species, nz), jnp.float32)
                return carry
            lax.fori_loop(0, ny // 2, fill, 0)

        @pl.when(jnp.logical_not(exists(0, sides[side])))
        def _(side=side):
            for t in range(SUBSTEPS):
                edge_from[t, side] = jnp.zeros((nx, species, nz), jnp.float32)

    for index in range(8):
        dx, dy = shifts[index]

        @pl.when(jnp.logical_not(exists(-dx, -dy)))
        def _(index=index, dx=dx, dy=dy):
            landing[index] = jnp.zeros(landing.shape[1:], jnp.float32)
            rows = pl.ds(1, bins_y) if dy == 0 else pl.ds(0 if dy > 0 else bins_y + 1, 1)
            count = bins_y if dy == 0 else 1
            pts[1 - dx, rows] = jnp.zeros((count,) + pts.shape[2:], jnp.float32)

    secreted().wait_recv()
    placed().wait_recv()
    depth = lax.broadcasted_iota(jnp.int32, (nz, lanes), 0)
    slot = lax.broadcasted_iota(jnp.int32, (1, lanes), 1)
    layer = slot // SLOTS
    ours = (slot // (lanes // 2)) == p
    for by in range(bins_y):
        place = jnp.where(ours, off_ref[0, by : by + 1, :], pltpu.roll(off_from[0, by : by + 1, :], lanes // 2, 1))
        wide = lax.broadcasted_iota(jnp.int32, (species, lanes), 1)
        amount = jnp.where((wide // (lanes // 2)) == p, sec_to[by], sec_from[by])
        amount = jnp.concatenate(split(amount), axis=0)
        cell = jnp.where(depth == layer * BIN_Z + (place & (BIN_Z - 1)), place >> 3, -1)

        def deposit(ox, carry, by=by, amount=amount, cell=cell):
            hits = jnp.concatenate(
                [
                    jnp.where(cell == ox * BIN_XY + oy, 1.0, 0.0).astype(jnp.bfloat16)
                    for oy in range(BIN_XY)
                ],
                axis=0,
            )
            total = lax.dot_general(
                amount, hits, (((1,), (1,)), ((), ())), preferred_element_type=jnp.float32
            )
            total = total[:species] + total[species:]
            for oy in range(BIN_XY):
                src[ox, by * BIN_XY + oy] = total[:, oy * nz : (oy + 1) * nz]
            return carry

        lax.fori_loop(0, BIN_XY, deposit, 0)

    mix_high, mix_low = split(mixing_ref[...] * time_step)
    mix = jnp.concatenate([mix_high, mix_high, mix_low], axis=1)
    diagonal = lax.broadcasted_iota(jnp.int32, (species, species), 0) == lax.broadcasted_iota(
        jnp.int32, (species, species), 1
    )
    reach = jnp.sum(jnp.where(diagonal, rates_ref[...], 0.0), axis=1, keepdims=True) * time_step
    keep = 1.0 - 6.0 * reach
    reach = jnp.broadcast_to(reach, (species, nz))
    keep = jnp.broadcast_to(keep, (species, nz))

    def gather_agents():
        for index in range(8):
            landed(agents(index), *shifts[index])
        for group in range(GROUPS):
            dx, dy = group // 3, group % 3
            for by in range(bins_y):
                row = group * bins_y + by
                for plane in range(4):
                    nb[plane, row : row + 1, :] = pts[dx, by + dy, plane : plane + 1, :]
                for plane in range(3):
                    own[plane, row : row + 1, :] = pts[1, by + 1, plane : plane + 1, :]
        used = GROUPS * bins_y
        if nb.shape[1] > used:
            for plane in range(4):
                nb[plane, used:, :] = jnp.zeros((nb.shape[1] - used, lanes), jnp.float32)
            for plane in range(3):
                own[plane, used:, :] = jnp.zeros((nb.shape[1] - used, lanes), jnp.float32)
        acc[...] = jnp.zeros(acc.shape, jnp.float32)

    span = 2 * SLOTS - 1

    def forces(first, last):
        def pair(d, carry):
            other = slot + d
            near = jnp.abs((other >> 4) - (slot >> 4)) <= 1
            near = jnp.logical_and(near, jnp.logical_and(other >= 0, other < lanes))
            turn = lax.rem(lanes - d, lanes)
            apart = [own[plane] - pltpu.roll(nb[plane], turn, 1) for plane in range(3)]
            heavy = jnp.where(near, pltpu.roll(nb[3], turn, 1), 0.0)
            square = apart[0] * apart[0] + apart[1] * apart[1] + apart[2] * apart[2]
            strength = heavy * jnp.exp(square * (-1.0 / spread_sq))
            for plane in range(3):
                acc[plane] += apart[plane] * strength
            return carry

        lax.fori_loop(first, last, pair, 0)

    def row_of(x, y):
        return (x if x in groups[1] else (1 if x == 0 else 2)) * ny - ny + y

    def show(t, x, half):
        side = 0 if x == 0 else 1
        for j in range(half * pairs, (half + 1) * pairs):
            even, odd = buf[t, x, 2 * j], buf[t, x, 2 * j + 1]
            if side == 0:
                face_to[t, side, j] = jnp.where(low, even, turned(odd))
            else:
                face_to[t, side, j] = jnp.where(low, turned(even), odd)
        send(face(t, side, half), 2 * sides[side], 0)

    def finish(t, group):
        for x in groups[group]:
            for side in range(2):
                send(edge(t, side, x), 0, sides[side])
        packed = jnp.zeros((species, nz), jnp.float32)
        for x in groups[group]:
            for y in range(ny):
                row = row_of(x, y)
                moved = pltpu.roll(buf[t, x, y], lax.rem(row + nz - rim, nz), 1)
                packed = jnp.where(inner == row, moved, packed)
        ends_to[t, group] = packed
        ends(t, group).start()

    def block(t, x, half):
        first = half * CHUNK
        cells = jnp.concatenate([buf[t, x, first + k] for k in range(CHUNK)], axis=1)
        high, less = split(cells)
        mixed = jnp.dot(
            mix, jnp.concatenate([high, less, high], axis=0), preferred_element_type=jnp.float32
        )
        beyond_z = ends_from[t, 0 if x in groups[0] else 1]
        for k in range(CHUNK):
            y = first + k
            here = buf[t, x, y]
            if x > 0:
                beside = buf[t, x - 1, y]
            elif y % 2 == 0:
                beside = jnp.where(low, face_from[t, 0, y // 2], turned(buf[t, nx - 1, y]))
            else:
                beside = turned(jnp.where(low, buf[t, nx - 1, y], face_from[t, 0, y // 2]))
            if x < nx - 1:
                beside = beside + buf[t, x + 1, y]
            elif y % 2 == 0:
                beside = beside + turned(jnp.where(low, face_from[t, 1, y // 2], buf[t, 0, y]))
            else:
                beside = beside + jnp.where(low, turned(buf[t, 0, y]), face_from[t, 1, y // 2])
            beside = beside + (edge_from[t, 0, x] if y == 0 else buf[t, x, y - 1])
            beside = beside + (edge_from[t, 1, x] if y == ny - 1 else buf[t, x, y + 1])
            beside = beside + jnp.where(inner == 0, 0.0, pltpu.roll(here, 1, 1))
            beside = beside + jnp.where(inner == mid - 1, 0.0, pltpu.roll(here, nz - 1, 1))
            arriving = pltpu.roll(beyond_z, lax.rem(rim + nz - row_of(x, y), nz), 1)
            beside = beside + jnp.where(inner == rim, arriving, 0.0)
            buf[t + 1, x, y] = (
                keep * here + reach * beside + mixed[:, k * nz : (k + 1) * nz] + src[x, y]
            )

    def hold(t, x):
        def put(y, value):
            buf[t, x, y] = value
        return put

    gather_agents()
    forces(-span, 0)
    for number, group in enumerate(groups):
        for half in range(halves):
            for x in group:
                enter(0, x, half, lambda y, x=x: home[x, y], hold(0, x))
                if number == 0:
                    show(0, x, half)
        finish(0, number)

    def substep(t, carry):
        for number, group in enumerate(groups):
            for x in group:
                for side in range(2):
                    landed(edge(t, side, x), 0, sides[side])
            ends(t, number).wait_recv()
            for half in range(halves):
                for x in group:
                    if number == 0:
                        side = 1 if x == 0 else 0
                        landed(face(t, side, half), 2 * sides[side], 0)
                    block(t, x, half)

                    @pl.when(t == SUBSTEPS - 1)
                    def _(x=x, half=half):
                        leave(1, x, half, lambda y, x=x: buf[SUBSTEPS, x, y])

                    if number == 0:
                        @pl.when(t < SUBSTEPS - 1)
                        def _(x=x, half=half):
                            show(t + 1, x, half)

            @pl.when(t < SUBSTEPS - 1)
            def _(number=number):
                finish(t + 1, number)

        return carry

    lax.fori_loop(0, SUBSTEPS, substep, 0)

    forces(0, span + 1)
    scale = move_step * alive
    for plane in range(3):
        force = acc[plane, 0:bins_y, :]
        for group in range(1, GROUPS):
            force = force + acc[plane, group * bins_y : (group + 1) * bins_y, :]
        disp_ref[plane, 0] = scale * force

    def store(x, half):
        rows = pl.ds(half * CHUNK, CHUNK)
        return pltpu.make_async_copy(home.at[x, rows], out_ref.at[x, rows], stored.at[x, half])

    for x, half in order:
        def put(y, value, x=x):
            home[x, y] = value

        enter(1, x, half, lambda y, x=x: buf[SUBSTEPS, x, y], put)
        store(x, half).start()

    for index in range(8):
        landed(migrants(index), *shifts[index])
        arrived_ref[:, index, :] = landing[index]
    secreted().wait_send()
    placed().wait_send()
    for index in range(8):
        sent(agents(index), *shifts[index])
        sent(migrants(index), *shifts[index])
    for x, half in order:
        swap(0, x, half).wait_send()
        swap(1, x, half).wait_send()

    def drain(t, carry):
        for side in range(2):
            for half in range(halves):
                sent(face(t, side, half), 2 * sides[side], 0)
            for x in range(nx):
                sent(edge(t, side, x), 0, sides[side])
        for number in range(2):
            ends(t, number).wait_send()
        return carry

    lax.fori_loop(0, SUBSTEPS, drain, 0)
    for x, half in order:
        store(x, half).wait()


def on_device(
    field, rates, mixing, secretion, positions, stiffness, occupancy, offsets, migrant_state, migrant_live
):
    species, nx, ny, nz = field.shape
    bins_y, lanes = stiffness.shape[1:]
    halves = ny // CHUNK
    kinds, state, slots = migrant_state.shape
    rows = -(-GROUPS * bins_y // 8) * 8
    cells = jnp.transpose(field, (1, 2, 0, 3))
    vmem = pl.BlockSpec(memory_space=pltpu.VMEM)
    anywhere = pl.BlockSpec(memory_space=pl.ANY)
    dma = pltpu.SemaphoreType.DMA
    result, moved, arrived = pl.pallas_call(
        kernel,
        out_shape=(
            jax.ShapeDtypeStruct(cells.shape, jnp.float32),
            jax.ShapeDtypeStruct(positions.shape, jnp.float32),
            jax.ShapeDtypeStruct((state, kinds, slots), jnp.float32),
        ),
        in_specs=[anywhere] + [vmem] * 9,
        out_specs=(anywhere, vmem, vmem),
        scratch_shapes=[
            pltpu.VMEM((nx, ny, species, nz), jnp.float32),
            pltpu.VMEM((SUBSTEPS + 1, nx, ny, species, nz), jnp.float32),
            pltpu.VMEM((2, nx, ny // 2, species, nz), jnp.float32),
            pltpu.VMEM((2, nx, ny // 2, species, nz), jnp.float32),
            pltpu.VMEM((SUBSTEPS, 2, ny // 2, species, nz), jnp.float32),
            pltpu.VMEM((SUBSTEPS, 2, ny // 2, species, nz), jnp.float32),
            pltpu.VMEM((SUBSTEPS, 2, nx, species, nz), jnp.float32),
            pltpu.VMEM((SUBSTEPS, 2, species, nz), jnp.float32),
            pltpu.VMEM((SUBSTEPS, 2, species, nz), jnp.float32),
            pltpu.VMEM((bins_y, species, lanes), jnp.float32),
            pltpu.VMEM((bins_y, species, lanes), jnp.float32),
            pltpu.VMEM(offsets.shape, jnp.int32),
            pltpu.VMEM((nx, ny, species, nz), jnp.float32),
            pltpu.VMEM((3, bins_y + 2, 8, lanes), jnp.float32),
            pltpu.VMEM((4, rows, lanes), jnp.float32),
            pltpu.VMEM((3, rows, lanes), jnp.float32),
            pltpu.VMEM((3, rows, lanes), jnp.float32),
            pltpu.VMEM(migrant_state.shape, jnp.float32),
            pltpu.VMEM(migrant_state.shape, jnp.float32),
            dma((2, nx, halves)),
            dma((2, nx, halves)),
            dma((SUBSTEPS, 2, halves)),
            dma((SUBSTEPS, 2, halves)),
            dma((SUBSTEPS, 2, nx)),
            dma((SUBSTEPS, 2, nx)),
            dma((SUBSTEPS, 2)),
            dma((SUBSTEPS, 2)),
            dma((2,)),
            dma((2,)),
            dma((8,)),
            dma((8,)),
            dma((8,)),
            dma((8,)),
            dma((1,)),
            dma((nx, halves)),
        ],
        compiler_params=pltpu.CompilerParams(
            collective_id=0, has_side_effects=True, vmem_limit_bytes=40 * 1024 * 1024
        ),
        name="tumour_step",
    )(
        cells,
        rates[None],
        mixing,
        secretion,
        positions,
        stiffness,
        occupancy,
        offsets,
        jnp.transpose(migrant_state, (1, 0, 2)),
        migrant_live,
    )
    return jnp.transpose(result, (2, 0, 1, 3)), moved, jnp.transpose(arrived, (1, 0, 2))


def solution(mesh):
    return jax.shard_map(
        on_device,
        mesh=mesh,
        in_specs=(
            P(None, "gx", "gy", None),
            P(),
            P(),
            P(None, "gx", "gy", None),
            P(None, "gx", "gy", None),
            P("gx", "gy", None),
            P("gx", "gy", None),
            P("gx", "gy", None),
            P(None, "gx", "gy"),
            P(None, "gx", "gy"),
        ),
        out_specs=(P(None, "gx", "gy", None), P(None, "gx", "gy", None), P(None, "gx", "gy")),
        check_vma=False,
    )
```

```python
import jax
import jax.numpy as jnp
from jax import lax
from jax.experimental import pallas as pl
from jax.experimental.pallas import tpu as pltpu
from jax.sharding import PartitionSpec as P

BIN_XY = 4
BIN_Z = 8
SLOTS = 16
SUBSTEPS = 4
CHUNK = 8
GROUPS = 9

time_step = 0.15
move_step = 0.1
spread_sq = 8.0
shifts = ((-1, -1), (-1, 0), (-1, 1), (0, -1), (0, 1), (1, -1), (1, 0), (1, 1))
MESH = pl.DeviceIdType.MESH


def split(value):
    high = value.astype(jnp.bfloat16)
    return high, (value - high.astype(jnp.float32)).astype(jnp.bfloat16)


def kernel(
    field_ref, rates_ref, mixing_ref, sec_ref, pos_ref, stiff_ref, occ_ref, off_ref, state_ref, live_ref,
    out_ref, disp_ref, arrived_ref,
    buf, swap_to, swap_from, face_to, face_from, edge_from, ends_to, ends_from,
    sec_to, sec_from, off_from, src, pts, nb, own, acc, payload, landing,
    s_swap, r_swap, s_face, r_face, s_edge, r_edge, s_ends, r_ends, s_sec, r_sec,
    s_pts, r_pts, s_mig, r_mig,
):
    species, nx, ny, nz = field_ref.shape
    bins_y, lanes = stiff_ref.shape[1:]
    halves = ny // CHUNK
    pairs = CHUNK // 2
    mid = nz // 2
    groups = ((0, nx - 1), tuple(range(1, nx - 1)))
    gx, gy = lax.axis_index("gx"), lax.axis_index("gy")
    n_gx, n_gy = lax.axis_size("gx"), lax.axis_size("gy")
    p = lax.rem(gx, 2)
    mate = (gx + 1 - 2 * p, gy)
    sides = (-1, 1)

    def exists(dx, dy):
        ok = None
        for coord, count, delta in ((gx, n_gx, dx), (gy, n_gy, dy)):
            if delta != 0:
                one = coord >= -delta if delta < 0 else coord < count - delta
                ok = one if ok is None else jnp.logical_and(ok, one)
        return ok

    barrier = pltpu.get_barrier_semaphore()
    for dx, dy in shifts + ((-2, 0), (2, 0)):
        @pl.when(exists(dx, dy))
        def _(dx=dx, dy=dy):
            pl.semaphore_signal(barrier, inc=1, device_id=(gx + dx, gy + dy), device_id_type=MESH)

    alive = occ_ref[0].astype(jnp.float32)
    weight = stiff_ref[0] * alive
    for by in range(bins_y):
        for plane in range(3):
            pts[1, by + 1, plane : plane + 1, :] = pos_ref[plane, 0, by : by + 1, :]
        pts[1, by + 1, 3:4, :] = weight[by : by + 1]
        sec_to[by] = sec_ref[:, 0, by, :] * (alive[by : by + 1] * time_step)

    column = lax.broadcasted_iota(jnp.int32, (species, nz), 1)
    kept = (column // mid) == p
    low = column < mid
    inner = column & (mid - 1)
    rim = (1 - p) * (mid - 1)

    def turned(value):
        return pltpu.roll(value, mid, 1)

    def remote(src_ref, dst_ref, send_sem, recv_sem, device):
        return pltpu.make_async_remote_copy(
            src_ref=src_ref,
            dst_ref=dst_ref,
            send_sem=send_sem,
            recv_sem=recv_sem,
            device_id=device,
            device_id_type=MESH,
        )

    def swap(way, x, half):
        rows = pl.ds(half * pairs, pairs)
        return remote(
            swap_to.at[way, x, rows], swap_from.at[way, x, rows],
            s_swap.at[way, x, half], r_swap.at[way, x, half], mate,
        )

    def face(t, side, half):
        rows = pl.ds(half * pairs, pairs)
        return remote(
            face_to.at[t, side, rows], face_from.at[t, 1 - side, rows],
            s_face.at[t, side, half], r_face.at[t, side, half], (gx + 2 * sides[side], gy),
        )

    def edge(t, side, x):
        return remote(
            buf.at[t, x, 0 if side == 0 else ny - 1], edge_from.at[t, 1 - side, x],
            s_edge.at[t, side, x], r_edge.at[t, side, x], (gx, gy + sides[side]),
        )

    def ends(t, group):
        return remote(
            ends_to.at[t, group], ends_from.at[t, group],
            s_ends.at[t, group], r_ends.at[t, group], mate,
        )

    def secreted():
        width = lanes // 2
        return remote(
            sec_to.at[:, :, pl.ds(pl.multiple_of((1 - p) * width, width), width)],
            sec_from.at[:, :, pl.ds(pl.multiple_of(p * width, width), width)],
            s_sec.at[0], r_sec.at[0], mate,
        )

    def placed():
        return remote(off_ref, off_from, s_sec.at[1], r_sec.at[1], mate)

    def agents(index):
        dx, dy = shifts[index]
        if dy == 0:
            mine, theirs = pl.ds(1, bins_y), pl.ds(1, bins_y)
        elif dy > 0:
            mine, theirs = pl.ds(bins_y, 1), pl.ds(0, 1)
        else:
            mine, theirs = pl.ds(1, 1), pl.ds(bins_y + 1, 1)
        return remote(
            pts.at[1, mine], pts.at[1 - dx, theirs],
            s_pts.at[index], r_pts.at[index], (gx + dx, gy + dy),
        )

    def migrants(index):
        dx, dy = shifts[index]
        return remote(
            payload.at[index], landing.at[index],
            s_mig.at[index], r_mig.at[index], (gx + dx, gy + dy),
        )

    def send(copy, dx, dy):
        @pl.when(exists(dx, dy))
        def _():
            copy.start()

    def landed(copy, dx, dy):
        @pl.when(exists(-dx, -dy))
        def _():
            copy.wait_recv()

    def sent(copy, dx, dy):
        @pl.when(exists(dx, dy))
        def _():
            copy.wait_send()

    def leave(way, x, half, cells):
        for j in range(half * pairs, (half + 1) * pairs):
            swap_to[way, x, j] = jnp.where(kept, turned(cells(2 * j)), cells(2 * j + 1))
        swap(way, x, half).start()

    def enter(way, x, half, cells, keep_in):
        swap(way, x, half).wait_recv()
        for j in range(half * pairs, (half + 1) * pairs):
            came = swap_from[way, x, j]
            keep_in(2 * j, jnp.where(kept, cells(2 * j), came))
            keep_in(2 * j + 1, jnp.where(kept, cells(2 * j + 1), turned(came)))

    across = 1 + (gx > 0).astype(jnp.int32) + (gx < n_gx - 1).astype(jnp.int32)
    along = 1 + (gy > 0).astype(jnp.int32) + (gy < n_gy - 1).astype(jnp.int32)
    beyond = (gx > 1).astype(jnp.int32) + (gx < n_gx - 2).astype(jnp.int32)
    pl.semaphore_wait(barrier, across * along - 1 + beyond)

    secreted().start()
    placed().start()
    order = [(x, half) for group in groups for half in range(halves) for x in group]
    for x, half in order:
        leave(0, x, half, lambda y, x=x: field_ref[:, x, y, :])
    for index in range(8):
        payload[index] = state_ref[:, index, :] * live_ref[index].astype(jnp.float32)

    for side in range(2):
        @pl.when(jnp.logical_not(exists(2 * sides[side], 0)))
        def _(side=side):
            def fill(row, carry):
                for t in range(SUBSTEPS):
                    face_from[t, side, row] = jnp.zeros((species, nz), jnp.float32)
                return carry
            lax.fori_loop(0, ny // 2, fill, 0)

        @pl.when(jnp.logical_not(exists(0, sides[side])))
        def _(side=side):
            for t in range(SUBSTEPS):
                edge_from[t, side] = jnp.zeros((nx, species, nz), jnp.float32)

    for index in range(8):
        dx, dy = shifts[index]

        @pl.when(jnp.logical_not(exists(-dx, -dy)))
        def _(index=index, dx=dx, dy=dy):
            landing[index] = jnp.zeros(landing.shape[1:], jnp.float32)
            rows = pl.ds(1, bins_y) if dy == 0 else pl.ds(0 if dy > 0 else bins_y + 1, 1)
            count = bins_y if dy == 0 else 1
            pts[1 - dx, rows] = jnp.zeros((count,) + pts.shape[2:], jnp.float32)

    secreted().wait_recv()
    placed().wait_recv()
    depth = lax.broadcasted_iota(jnp.int32, (nz, lanes), 0)
    slot = lax.broadcasted_iota(jnp.int32, (1, lanes), 1)
    layer = slot // SLOTS
    ours = (slot // (lanes // 2)) == p
    for by in range(bins_y):
        place = jnp.where(ours, off_ref[0, by : by + 1, :], pltpu.roll(off_from[0, by : by + 1, :], lanes // 2, 1))
        wide = lax.broadcasted_iota(jnp.int32, (species, lanes), 1)
        amount = jnp.where((wide // (lanes // 2)) == p, sec_to[by], sec_from[by])
        amount = jnp.concatenate(split(amount), axis=0)
        cell = jnp.where(depth == layer * BIN_Z + (place & (BIN_Z - 1)), place >> 3, -1)

        def deposit(ox, carry, by=by, amount=amount, cell=cell):
            hits = jnp.concatenate(
                [
                    jnp.where(cell == ox * BIN_XY + oy, 1.0, 0.0).astype(jnp.bfloat16)
                    for oy in range(BIN_XY)
                ],
                axis=0,
            )
            total = lax.dot_general(
                amount, hits, (((1,), (1,)), ((), ())), preferred_element_type=jnp.float32
            )
            total = total[:species] + total[species:]
            for oy in range(BIN_XY):
                src[ox, by * BIN_XY + oy] = total[:, oy * nz : (oy + 1) * nz]
            return carry

        lax.fori_loop(0, BIN_XY, deposit, 0)

    mix_high, mix_low = split(mixing_ref[...] * time_step)
    mix = jnp.concatenate([mix_high, mix_high, mix_low], axis=1)
    diagonal = lax.broadcasted_iota(jnp.int32, (species, species), 0) == lax.broadcasted_iota(
        jnp.int32, (species, species), 1
    )
    reach = jnp.sum(jnp.where(diagonal, rates_ref[...], 0.0), axis=1, keepdims=True) * time_step
    keep = 1.0 - 6.0 * reach
    reach = jnp.broadcast_to(reach, (species, nz))
    keep = jnp.broadcast_to(keep, (species, nz))

    def gather_agents():
        for index in range(8):
            landed(agents(index), *shifts[index])
        for group in range(GROUPS):
            dx, dy = group // 3, group % 3
            for by in range(bins_y):
                row = group * bins_y + by
                for plane in range(4):
                    nb[plane, row : row + 1, :] = pts[dx, by + dy, plane : plane + 1, :]
                for plane in range(3):
                    own[plane, row : row + 1, :] = pts[1, by + 1, plane : plane + 1, :]
        used = GROUPS * bins_y
        if nb.shape[1] > used:
            for plane in range(4):
                nb[plane, used:, :] = jnp.zeros((nb.shape[1] - used, lanes), jnp.float32)
            for plane in range(3):
                own[plane, used:, :] = jnp.zeros((nb.shape[1] - used, lanes), jnp.float32)
        acc[...] = jnp.zeros(acc.shape, jnp.float32)

    span = 2 * SLOTS - 1

    def forces(first, last):
        def pair(d, carry):
            other = slot + d
            near = jnp.abs((other >> 4) - (slot >> 4)) <= 1
            near = jnp.logical_and(near, jnp.logical_and(other >= 0, other < lanes))
            turn = lax.rem(lanes - d, lanes)
            apart = [own[plane] - pltpu.roll(nb[plane], turn, 1) for plane in range(3)]
            heavy = jnp.where(near, pltpu.roll(nb[3], turn, 1), 0.0)
            square = apart[0] * apart[0] + apart[1] * apart[1] + apart[2] * apart[2]
            strength = heavy * jnp.exp(square * (-1.0 / spread_sq))
            for plane in range(3):
                acc[plane] += apart[plane] * strength
            return carry

        lax.fori_loop(first, last, pair, 0)

    def row_of(x, y):
        return (x if x in groups[1] else (1 if x == 0 else 2)) * ny - ny + y

    def show(t, x, half):
        side = 0 if x == 0 else 1
        for j in range(half * pairs, (half + 1) * pairs):
            even, odd = buf[t, x, 2 * j], buf[t, x, 2 * j + 1]
            if side == 0:
                face_to[t, side, j] = jnp.where(low, even, turned(odd))
            else:
                face_to[t, side, j] = jnp.where(low, turned(even), odd)
        send(face(t, side, half), 2 * sides[side], 0)

    def finish(t, group):
        for x in groups[group]:
            for side in range(2):
                send(edge(t, side, x), 0, sides[side])
        packed = jnp.zeros((species, nz), jnp.float32)
        for x in groups[group]:
            for y in range(ny):
                row = row_of(x, y)
                moved = pltpu.roll(buf[t, x, y], lax.rem(row + nz - rim, nz), 1)
                packed = jnp.where(inner == row, moved, packed)
        ends_to[t, group] = packed
        ends(t, group).start()

    def block(t, x, half):
        first = half * CHUNK
        cells = jnp.concatenate([buf[t, x, first + k] for k in range(CHUNK)], axis=1)
        high, less = split(cells)
        mixed = jnp.dot(
            mix, jnp.concatenate([high, less, high], axis=0), preferred_element_type=jnp.float32
        )
        beyond_z = ends_from[t, 0 if x in groups[0] else 1]
        for k in range(CHUNK):
            y = first + k
            here = buf[t, x, y]
            if x > 0:
                beside = buf[t, x - 1, y]
            elif y % 2 == 0:
                beside = jnp.where(low, face_from[t, 0, y // 2], turned(buf[t, nx - 1, y]))
            else:
                beside = turned(jnp.where(low, buf[t, nx - 1, y], face_from[t, 0, y // 2]))
            if x < nx - 1:
                beside = beside + buf[t, x + 1, y]
            elif y % 2 == 0:
                beside = beside + turned(jnp.where(low, face_from[t, 1, y // 2], buf[t, 0, y]))
            else:
                beside = beside + jnp.where(low, turned(buf[t, 0, y]), face_from[t, 1, y // 2])
            beside = beside + (edge_from[t, 0, x] if y == 0 else buf[t, x, y - 1])
            beside = beside + (edge_from[t, 1, x] if y == ny - 1 else buf[t, x, y + 1])
            beside = beside + jnp.where(inner == 0, 0.0, pltpu.roll(here, 1, 1))
            beside = beside + jnp.where(inner == mid - 1, 0.0, pltpu.roll(here, nz - 1, 1))
            arriving = pltpu.roll(beyond_z, lax.rem(rim + nz - row_of(x, y), nz), 1)
            beside = beside + jnp.where(inner == rim, arriving, 0.0)
            buf[t + 1, x, y] = (
                keep * here + reach * beside + mixed[:, k * nz : (k + 1) * nz] + src[x, y]
            )

    def hold(t, x):
        def put(y, value):
            buf[t, x, y] = value
        return put

    for number, group in enumerate(groups):
        for half in range(halves):
            for x in group:
                enter(0, x, half, lambda y, x=x: field_ref[:, x, y, :], hold(0, x))
                if number == 0:
                    show(0, x, half)
        finish(0, number)
    for index in range(8):
        send(agents(index), *shifts[index])
    for index in range(8):
        send(migrants(index), *shifts[index])

    def substep(t, carry):
        for number, group in enumerate(groups):
            for x in group:
                for side in range(2):
                    landed(edge(t, side, x), 0, sides[side])
            ends(t, number).wait_recv()
            for half in range(halves):
                for x in group:
                    if number == 0:
                        side = 1 if x == 0 else 0
                        landed(face(t, side, half), 2 * sides[side], 0)
                    block(t, x, half)

                    @pl.when(t == SUBSTEPS - 1)
                    def _(x=x, half=half):
                        leave(1, x, half, lambda y, x=x: buf[SUBSTEPS, x, y])

                    if number == 0:
                        @pl.when(t < SUBSTEPS - 1)
                        def _(x=x, half=half):
                            show(t + 1, x, half)

            @pl.when(t < SUBSTEPS - 1)
            def _(number=number):
                finish(t + 1, number)

        return carry

    lax.fori_loop(0, SUBSTEPS, substep, 0)

    gather_agents()
    forces(-span, 0)
    forces(0, span + 1)
    scale = move_step * alive
    for plane in range(3):
        force = acc[plane, 0:bins_y, :]
        for group in range(1, GROUPS):
            force = force + acc[plane, group * bins_y : (group + 1) * bins_y, :]
        disp_ref[plane, 0] = scale * force

    for x, half in order:
        def put(y, value, x=x):
            out_ref[:, x, y, :] = value

        enter(1, x, half, lambda y, x=x: buf[SUBSTEPS, x, y], put)

    for index in range(8):
        landed(migrants(index), *shifts[index])
        arrived_ref[:, index, :] = landing[index]
    secreted().wait_send()
    placed().wait_send()
    for index in range(8):
        sent(agents(index), *shifts[index])
        sent(migrants(index), *shifts[index])
    for x, half in order:
        swap(0, x, half).wait_send()
        swap(1, x, half).wait_send()

    def drain(t, carry):
        for side in range(2):
            for half in range(halves):
                sent(face(t, side, half), 2 * sides[side], 0)
            for x in range(nx):
                sent(edge(t, side, x), 0, sides[side])
        for number in range(2):
            ends(t, number).wait_send()
        return carry

    lax.fori_loop(0, SUBSTEPS, drain, 0)


def on_device(
    field, rates, mixing, secretion, positions, stiffness, occupancy, offsets, migrant_state, migrant_live
):
    species, nx, ny, nz = field.shape
    bins_y, lanes = stiffness.shape[1:]
    halves = ny // CHUNK
    kinds, state, slots = migrant_state.shape
    rows = -(-GROUPS * bins_y // 8) * 8
    vmem = pl.BlockSpec(memory_space=pltpu.VMEM)
    dma = pltpu.SemaphoreType.DMA
    result, moved, arrived = pl.pallas_call(
        kernel,
        out_shape=(
            jax.ShapeDtypeStruct(field.shape, jnp.float32),
            jax.ShapeDtypeStruct(positions.shape, jnp.float32),
            jax.ShapeDtypeStruct((state, kinds, slots), jnp.float32),
        ),
        in_specs=[vmem] * 10,
        out_specs=(vmem, vmem, vmem),
        scratch_shapes=[
            pltpu.VMEM((SUBSTEPS + 1, nx, ny, species, nz), jnp.float32),
            pltpu.VMEM((2, nx, ny // 2, species, nz), jnp.float32),
            pltpu.VMEM((2, nx, ny // 2, species, nz), jnp.float32),
            pltpu.VMEM((SUBSTEPS, 2, ny // 2, species, nz), jnp.float32),
            pltpu.VMEM((SUBSTEPS, 2, ny // 2, species, nz), jnp.float32),
            pltpu.VMEM((SUBSTEPS, 2, nx, species, nz), jnp.float32),
            pltpu.VMEM((SUBSTEPS, 2, species, nz), jnp.float32),
            pltpu.VMEM((SUBSTEPS, 2, species, nz), jnp.float32),
            pltpu.VMEM((bins_y, species, lanes), jnp.float32),
            pltpu.VMEM((bins_y, species, lanes), jnp.float32),
            pltpu.VMEM(offsets.shape, jnp.int32),
            pltpu.VMEM((nx, ny, species, nz), jnp.float32),
            pltpu.VMEM((3, bins_y + 2, 8, lanes), jnp.float32),
            pltpu.VMEM((4, rows, lanes), jnp.float32),
            pltpu.VMEM((3, rows, lanes), jnp.float32),
            pltpu.VMEM((3, rows, lanes), jnp.float32),
            pltpu.VMEM(migrant_state.shape, jnp.float32),
            pltpu.VMEM(migrant_state.shape, jnp.float32),
            dma((2, nx, halves)),
            dma((2, nx, halves)),
            dma((SUBSTEPS, 2, halves)),
            dma((SUBSTEPS, 2, halves)),
            dma((SUBSTEPS, 2, nx)),
            dma((SUBSTEPS, 2, nx)),
            dma((SUBSTEPS, 2)),
            dma((SUBSTEPS, 2)),
            dma((2,)),
            dma((2,)),
            dma((8,)),
            dma((8,)),
            dma((8,)),
            dma((8,)),
        ],
        compiler_params=pltpu.CompilerParams(
            collective_id=0, has_side_effects=True, vmem_limit_bytes=40 * 1024 * 1024
        ),
        name="tumour_step",
    )(
        field,
        rates[None],
        mixing,
        secretion,
        positions,
        stiffness,
        occupancy,
        offsets,
        jnp.transpose(migrant_state, (1, 0, 2)),
        migrant_live,
    )
    return result, moved, jnp.transpose(arrived, (1, 0, 2))


def solution(mesh):
    return jax.shard_map(
        on_device,
        mesh=mesh,
        in_specs=(
            P(None, "gx", "gy", None),
            P(),
            P(),
            P(None, "gx", "gy", None),
            P(None, "gx", "gy", None),
            P("gx", "gy", None),
            P("gx", "gy", None),
            P("gx", "gy", None),
            P(None, "gx", "gy"),
            P(None, "gx", "gy"),
        ),
        out_specs=(P(None, "gx", "gy", None), P(None, "gx", "gy", None), P(None, "gx", "gy")),
        check_vma=False,
    )
```

```python
import jax
import jax.numpy as jnp
from jax import lax
from jax.experimental import pallas as pl
from jax.experimental.pallas import tpu as pltpu
from jax.sharding import PartitionSpec as P

BIN_XY = 4
BIN_Z = 8
SLOTS = 16
SUBSTEPS = 4
CHUNK = 8
GROUPS = 9
GRANT = 56 * 1024 * 1024
PIECES = 4

time_step = 0.15
move_step = 0.1
spread_sq = 8.0
shifts = ((-1, -1), (-1, 0), (-1, 1), (0, -1), (0, 1), (1, -1), (1, 0), (1, 1))
MESH = pl.DeviceIdType.MESH


def split(value):
    high = value.astype(jnp.bfloat16)
    return high, (value - high.astype(jnp.float32)).astype(jnp.bfloat16)


def kernel(
    field_in, rates_in, mixing_in, sec_in, pos_in, stiff_in, occ_in, off_in, state_in, live_in,
    out_ref, disp_ref, arrived_ref,
    field_ref, rates_ref, mixing_ref, sec_ref, pos_ref, stiff_ref, occ_ref, off_ref, state_ref, live_ref,
    s_load,
    buf, swap_to, swap_from, face_to, face_from, edge_from, ends_to, ends_from,
    sec_to, sec_from, off_from, src, pts, nb, own, acc, payload, landing,
    s_swap, r_swap, s_face, r_face, s_edge, r_edge, s_ends, r_ends, s_sec, r_sec,
    s_pts, r_pts, s_mig, r_mig,
):
    species, nx, ny, nz = field_ref.shape
    bins_y, lanes = stiff_ref.shape[1:]
    halves = ny // CHUNK
    pairs = CHUNK // 2
    mid = nz // 2
    groups = ((0, nx - 1), tuple(range(1, nx - 1)))
    gx, gy = lax.axis_index("gx"), lax.axis_index("gy")
    n_gx, n_gy = lax.axis_size("gx"), lax.axis_size("gy")
    p = lax.rem(gx, 2)
    mate = (gx + 1 - 2 * p, gy)
    sides = (-1, 1)

    def exists(dx, dy):
        ok = None
        for coord, count, delta in ((gx, n_gx, dx), (gy, n_gy, dy)):
            if delta != 0:
                one = coord >= -delta if delta < 0 else coord < count - delta
                ok = one if ok is None else jnp.logical_and(ok, one)
        return ok

    loads = [
        pltpu.make_async_copy(there, here, s_load.at[place])
        for place, (there, here) in enumerate(
            (
                (sec_in, sec_ref),
                (occ_in, occ_ref),
                (stiff_in, stiff_ref),
                (pos_in, pos_ref),
                (off_in, off_ref),
                (field_in, field_ref),
                (state_in, state_ref),
                (live_in, live_ref),
                (rates_in, rates_ref),
                (mixing_in, mixing_ref),
            )
        )
    ]
    for load in loads:
        load.start()

    barrier = pltpu.get_barrier_semaphore()
    for dx, dy in shifts + ((-2, 0), (2, 0)):
        @pl.when(exists(dx, dy))
        def _(dx=dx, dy=dy):
            pl.semaphore_signal(barrier, inc=1, device_id=(gx + dx, gy + dy), device_id_type=MESH)

    for load in loads[:5]:
        load.wait()
    alive = occ_ref[0].astype(jnp.float32)
    weight = stiff_ref[0] * alive
    for by in range(bins_y):
        for plane in range(3):
            pts[1, by + 1, plane : plane + 1, :] = pos_ref[plane, 0, by : by + 1, :]
        pts[1, by + 1, 3:4, :] = weight[by : by + 1]
        sec_to[by] = sec_ref[:, 0, by, :] * (alive[by : by + 1] * time_step)

    column = lax.broadcasted_iota(jnp.int32, (species, nz), 1)
    kept = (column // mid) == p
    low = column < mid
    inner = column & (mid - 1)
    rim = (1 - p) * (mid - 1)

    def turned(value):
        return pltpu.roll(value, mid, 1)

    def remote(src_ref, dst_ref, send_sem, recv_sem, device):
        return pltpu.make_async_remote_copy(
            src_ref=src_ref,
            dst_ref=dst_ref,
            send_sem=send_sem,
            recv_sem=recv_sem,
            device_id=device,
            device_id_type=MESH,
        )

    def swap(way, x, half):
        rows = pl.ds(half * pairs, pairs)
        return remote(
            swap_to.at[way, x, rows], swap_from.at[way, x, rows],
            s_swap.at[way, x, half], r_swap.at[way, x, half], mate,
        )

    def face(t, side, half):
        rows = pl.ds(half * pairs, pairs)
        return remote(
            face_to.at[t, side, rows], face_from.at[t, 1 - side, rows],
            s_face.at[t, side, half], r_face.at[t, side, half], (gx + 2 * sides[side], gy),
        )

    def edge(t, side, x):
        return remote(
            buf.at[t, x, 0 if side == 0 else ny - 1], edge_from.at[t, 1 - side, x],
            s_edge.at[t, side, x], r_edge.at[t, side, x], (gx, gy + sides[side]),
        )

    def ends(t, group):
        return remote(
            ends_to.at[t, group], ends_from.at[t, group],
            s_ends.at[t, group], r_ends.at[t, group], mate,
        )

    def secreted():
        width = lanes // 2
        return remote(
            sec_to.at[:, :, pl.ds(pl.multiple_of((1 - p) * width, width), width)],
            sec_from.at[:, :, pl.ds(pl.multiple_of(p * width, width), width)],
            s_sec.at[0], r_sec.at[0], mate,
        )

    def placed():
        return remote(off_ref, off_from, s_sec.at[1], r_sec.at[1], mate)

    def agents(index):
        dx, dy = shifts[index]
        if dy == 0:
            mine, theirs = pl.ds(1, bins_y), pl.ds(1, bins_y)
        elif dy > 0:
            mine, theirs = pl.ds(bins_y, 1), pl.ds(0, 1)
        else:
            mine, theirs = pl.ds(1, 1), pl.ds(bins_y + 1, 1)
        return remote(
            pts.at[1, mine], pts.at[1 - dx, theirs],
            s_pts.at[index], r_pts.at[index], (gx + dx, gy + dy),
        )

    def migrants(index):
        dx, dy = shifts[index]
        return remote(
            payload.at[index], landing.at[index],
            s_mig.at[index], r_mig.at[index], (gx + dx, gy + dy),
        )

    def send(copy, dx, dy):
        @pl.when(exists(dx, dy))
        def _():
            copy.start()

    def landed(copy, dx, dy):
        @pl.when(exists(-dx, -dy))
        def _():
            copy.wait_recv()

    def sent(copy, dx, dy):
        @pl.when(exists(dx, dy))
        def _():
            copy.wait_send()

    def leave(way, x, half, cells):
        for j in range(half * pairs, (half + 1) * pairs):
            swap_to[way, x, j] = jnp.where(kept, turned(cells(2 * j)), cells(2 * j + 1))
        swap(way, x, half).start()

    def enter(way, x, half, cells, keep_in):
        swap(way, x, half).wait_recv()
        for j in range(half * pairs, (half + 1) * pairs):
            came = swap_from[way, x, j]
            keep_in(2 * j, jnp.where(kept, cells(2 * j), came))
            keep_in(2 * j + 1, jnp.where(kept, cells(2 * j + 1), turned(came)))

    across = 1 + (gx > 0).astype(jnp.int32) + (gx < n_gx - 1).astype(jnp.int32)
    along = 1 + (gy > 0).astype(jnp.int32) + (gy < n_gy - 1).astype(jnp.int32)
    beyond = (gx > 1).astype(jnp.int32) + (gx < n_gx - 2).astype(jnp.int32)
    pl.semaphore_wait(barrier, across * along - 1 + beyond)

    secreted().start()
    placed().start()
    for load in loads[5:]:
        load.wait()
    order = [(x, half) for group in groups for half in range(halves) for x in group]
    for x, half in order:
        leave(0, x, half, lambda y, x=x: field_ref[:, x, y, :])
    for index in range(8):
        payload[index] = state_ref[:, index, :] * live_ref[index].astype(jnp.float32)

    for side in range(2):
        @pl.when(jnp.logical_not(exists(2 * sides[side], 0)))
        def _(side=side):
            def fill(row, carry):
                for t in range(SUBSTEPS):
                    face_from[t, side, row] = jnp.zeros((species, nz), jnp.float32)
                return carry
            lax.fori_loop(0, ny // 2, fill, 0)

        @pl.when(jnp.logical_not(exists(0, sides[side])))
        def _(side=side):
            for t in range(SUBSTEPS):
                edge_from[t, side] = jnp.zeros((nx, species, nz), jnp.float32)

    for index in range(8):
        dx, dy = shifts[index]

        @pl.when(jnp.logical_not(exists(-dx, -dy)))
        def _(index=index, dx=dx, dy=dy):
            landing[index] = jnp.zeros(landing.shape[1:], jnp.float32)
            rows = pl.ds(1, bins_y) if dy == 0 else pl.ds(0 if dy > 0 else bins_y + 1, 1)
            count = bins_y if dy == 0 else 1
            pts[1 - dx, rows] = jnp.zeros((count,) + pts.shape[2:], jnp.float32)

    secreted().wait_recv()
    placed().wait_recv()
    depth = lax.broadcasted_iota(jnp.int32, (nz, lanes), 0)
    slot = lax.broadcasted_iota(jnp.int32, (1, lanes), 1)
    layer = slot // SLOTS
    ours = (slot // (lanes // 2)) == p
    for by in range(bins_y):
        place = jnp.where(ours, off_ref[0, by : by + 1, :], pltpu.roll(off_from[0, by : by + 1, :], lanes // 2, 1))
        wide = lax.broadcasted_iota(jnp.int32, (species, lanes), 1)
        amount = jnp.where((wide // (lanes // 2)) == p, sec_to[by], sec_from[by])
        amount = jnp.concatenate(split(amount), axis=0)
        cell = jnp.where(depth == layer * BIN_Z + (place & (BIN_Z - 1)), place >> 3, -1)

        def deposit(ox, carry, by=by, amount=amount, cell=cell):
            hits = jnp.concatenate(
                [
                    jnp.where(cell == ox * BIN_XY + oy, 1.0, 0.0).astype(jnp.bfloat16)
                    for oy in range(BIN_XY)
                ],
                axis=0,
            )
            total = lax.dot_general(
                amount, hits, (((1,), (1,)), ((), ())), preferred_element_type=jnp.float32
            )
            total = total[:species] + total[species:]
            for oy in range(BIN_XY):
                src[ox, by * BIN_XY + oy] = total[:, oy * nz : (oy + 1) * nz]
            return carry

        lax.fori_loop(0, BIN_XY, deposit, 0)

    mix_high, mix_low = split(mixing_ref[...] * time_step)
    mix = jnp.concatenate([mix_high, mix_high, mix_low], axis=1)
    diagonal = lax.broadcasted_iota(jnp.int32, (species, species), 0) == lax.broadcasted_iota(
        jnp.int32, (species, species), 1
    )
    reach = jnp.sum(jnp.where(diagonal, rates_ref[...], 0.0), axis=1, keepdims=True) * time_step
    keep = 1.0 - 6.0 * reach
    reach = jnp.broadcast_to(reach, (species, nz))
    keep = jnp.broadcast_to(keep, (species, nz))

    def gather_agents():
        for index in range(8):
            landed(agents(index), *shifts[index])
        for group in range(GROUPS):
            dx, dy = group // 3, group % 3
            for by in range(bins_y):
                row = group * bins_y + by
                for plane in range(4):
                    nb[plane, row : row + 1, :] = pts[dx, by + dy, plane : plane + 1, :]
                for plane in range(3):
                    own[plane, row : row + 1, :] = pts[1, by + 1, plane : plane + 1, :]
        used = GROUPS * bins_y
        if nb.shape[1] > used:
            for plane in range(4):
                nb[plane, used:, :] = jnp.zeros((nb.shape[1] - used, lanes), jnp.float32)
            for plane in range(3):
                own[plane, used:, :] = jnp.zeros((nb.shape[1] - used, lanes), jnp.float32)
        acc[...] = jnp.zeros(acc.shape, jnp.float32)

    span = 2 * SLOTS - 1

    def forces(first, last):
        def pair(d, carry):
            other = slot + d
            near = jnp.abs((other >> 4) - (slot >> 4)) <= 1
            near = jnp.logical_and(near, jnp.logical_and(other >= 0, other < lanes))
            turn = lax.rem(lanes - d, lanes)
            apart = [own[plane] - pltpu.roll(nb[plane], turn, 1) for plane in range(3)]
            heavy = jnp.where(near, pltpu.roll(nb[3], turn, 1), 0.0)
            square = apart[0] * apart[0] + apart[1] * apart[1] + apart[2] * apart[2]
            strength = heavy * jnp.exp(square * (-1.0 / spread_sq))
            for plane in range(3):
                acc[plane] += apart[plane] * strength
            return carry

        lax.fori_loop(first, last, pair, 0)

    def row_of(x, y):
        return (x if x in groups[1] else (1 if x == 0 else 2)) * ny - ny + y

    def show(t, x, half):
        side = 0 if x == 0 else 1
        for j in range(half * pairs, (half + 1) * pairs):
            even, odd = buf[t, x, 2 * j], buf[t, x, 2 * j + 1]
            if side == 0:
                face_to[t, side, j] = jnp.where(low, even, turned(odd))
            else:
                face_to[t, side, j] = jnp.where(low, turned(even), odd)
        send(face(t, side, half), 2 * sides[side], 0)

    def finish(t, group):
        for x in groups[group]:
            for side in range(2):
                send(edge(t, side, x), 0, sides[side])
        packed = jnp.zeros((species, nz), jnp.float32)
        for x in groups[group]:
            for y in range(ny):
                row = row_of(x, y)
                moved = pltpu.roll(buf[t, x, y], lax.rem(row + nz - rim, nz), 1)
                packed = jnp.where(inner == row, moved, packed)
        ends_to[t, group] = packed
        ends(t, group).start()

    def block(t, x, half):
        first = half * CHUNK
        cells = jnp.concatenate([buf[t, x, first + k] for k in range(CHUNK)], axis=1)
        high, less = split(cells)
        mixed = jnp.dot(
            mix, jnp.concatenate([high, less, high], axis=0), preferred_element_type=jnp.float32
        )
        beyond_z = ends_from[t, 0 if x in groups[0] else 1]
        for k in range(CHUNK):
            y = first + k
            here = buf[t, x, y]
            if x > 0:
                beside = buf[t, x - 1, y]
            elif y % 2 == 0:
                beside = jnp.where(low, face_from[t, 0, y // 2], turned(buf[t, nx - 1, y]))
            else:
                beside = turned(jnp.where(low, buf[t, nx - 1, y], face_from[t, 0, y // 2]))
            if x < nx - 1:
                beside = beside + buf[t, x + 1, y]
            elif y % 2 == 0:
                beside = beside + turned(jnp.where(low, face_from[t, 1, y // 2], buf[t, 0, y]))
            else:
                beside = beside + jnp.where(low, turned(buf[t, 0, y]), face_from[t, 1, y // 2])
            beside = beside + (edge_from[t, 0, x] if y == 0 else buf[t, x, y - 1])
            beside = beside + (edge_from[t, 1, x] if y == ny - 1 else buf[t, x, y + 1])
            beside = beside + jnp.where(inner == 0, 0.0, pltpu.roll(here, 1, 1))
            beside = beside + jnp.where(inner == mid - 1, 0.0, pltpu.roll(here, nz - 1, 1))
            arriving = pltpu.roll(beyond_z, lax.rem(rim + nz - row_of(x, y), nz), 1)
            beside = beside + jnp.where(inner == rim, arriving, 0.0)
            buf[t + 1, x, y] = (
                keep * here + reach * beside + mixed[:, k * nz : (k + 1) * nz] + src[x, y]
            )

    def hold(t, x):
        def put(y, value):
            buf[t, x, y] = value
        return put

    for number, group in enumerate(groups):
        for half in range(halves):
            for x in group:
                enter(0, x, half, lambda y, x=x: field_ref[:, x, y, :], hold(0, x))
                if number == 0:
                    show(0, x, half)
        finish(0, number)
    for index in range(8):
        send(agents(index), *shifts[index])
    for index in range(8):
        send(migrants(index), *shifts[index])

    def substep(t, carry):
        for number, group in enumerate(groups):
            for x in group:
                for side in range(2):
                    landed(edge(t, side, x), 0, sides[side])
            ends(t, number).wait_recv()
            for half in range(halves):
                for x in group:
                    if number == 0:
                        side = 1 if x == 0 else 0
                        landed(face(t, side, half), 2 * sides[side], 0)
                    block(t, x, half)

                    @pl.when(t == SUBSTEPS - 1)
                    def _(x=x, half=half):
                        leave(1, x, half, lambda y, x=x: buf[SUBSTEPS, x, y])

                    if number == 0:
                        @pl.when(t < SUBSTEPS - 1)
                        def _(x=x, half=half):
                            show(t + 1, x, half)

            @pl.when(t < SUBSTEPS - 1)
            def _(number=number):
                finish(t + 1, number)

        return carry

    lax.fori_loop(0, SUBSTEPS, substep, 0)

    gather_agents()
    forces(-span, 0)
    forces(0, span + 1)
    scale = move_step * alive
    for plane in range(3):
        force = acc[plane, 0:bins_y, :]
        for group in range(1, GROUPS):
            force = force + acc[plane, group * bins_y : (group + 1) * bins_y, :]
        disp_ref[plane, 0] = scale * force

    for x, half in order:
        def put(y, value, x=x):
            out_ref[:, x, y, :] = value

        enter(1, x, half, lambda y, x=x: buf[SUBSTEPS, x, y], put)

    for index in range(8):
        landed(migrants(index), *shifts[index])
        arrived_ref[:, index, :] = landing[index]
    secreted().wait_send()
    placed().wait_send()
    for index in range(8):
        sent(agents(index), *shifts[index])
        sent(migrants(index), *shifts[index])
    for x, half in order:
        swap(0, x, half).wait_send()
        swap(1, x, half).wait_send()

    def drain(t, carry):
        for side in range(2):
            for half in range(halves):
                sent(face(t, side, half), 2 * sides[side], 0)
            for x in range(nx):
                sent(edge(t, side, x), 0, sides[side])
        for number in range(2):
            ends(t, number).wait_send()
        return carry

    lax.fori_loop(0, SUBSTEPS, drain, 0)


def on_device(
    field, rates, mixing, secretion, positions, stiffness, occupancy, offsets, migrant_state, migrant_live
):
    species, nx, ny, nz = field.shape
    bins_y, lanes = stiffness.shape[1:]
    halves = ny // CHUNK
    kinds, state, slots = migrant_state.shape
    rows = -(-GROUPS * bins_y // 8) * 8
    vmem = pl.BlockSpec(memory_space=pltpu.VMEM)
    hbm = pl.BlockSpec(memory_space=pltpu.HBM)
    inputs = (
        field,
        rates[None],
        mixing,
        secretion,
        positions,
        stiffness,
        occupancy,
        offsets,
        jnp.transpose(migrant_state, (1, 0, 2)),
        migrant_live,
    )
    dma = pltpu.SemaphoreType.DMA
    result, moved, arrived = pl.pallas_call(
        kernel,
        out_shape=(
            jax.ShapeDtypeStruct(field.shape, jnp.float32),
            jax.ShapeDtypeStruct(positions.shape, jnp.float32),
            jax.ShapeDtypeStruct((state, kinds, slots), jnp.float32),
        ),
        in_specs=[hbm] * 10,
        out_specs=(vmem, vmem, vmem),
        scratch_shapes=[pltpu.VMEM(value.shape, value.dtype) for value in inputs]
        + [
            dma((10,)),
            pltpu.VMEM((SUBSTEPS + 1, nx, ny, species, nz), jnp.float32),
            pltpu.VMEM((2, nx, ny // 2, species, nz), jnp.float32),
            pltpu.VMEM((2, nx, ny // 2, species, nz), jnp.float32),
            pltpu.VMEM((SUBSTEPS, 2, ny // 2, species, nz), jnp.float32),
            pltpu.VMEM((SUBSTEPS, 2, ny // 2, species, nz), jnp.float32),
            pltpu.VMEM((SUBSTEPS, 2, nx, species, nz), jnp.float32),
            pltpu.VMEM((SUBSTEPS, 2, species, nz), jnp.float32),
            pltpu.VMEM((SUBSTEPS, 2, species, nz), jnp.float32),
            pltpu.VMEM((bins_y, species, lanes), jnp.float32),
            pltpu.VMEM((bins_y, species, lanes), jnp.float32),
            pltpu.VMEM(offsets.shape, jnp.int32),
            pltpu.VMEM((nx, ny, species, nz), jnp.float32),
            pltpu.VMEM((3, bins_y + 2, 8, lanes), jnp.float32),
            pltpu.VMEM((4, rows, lanes), jnp.float32),
            pltpu.VMEM((3, rows, lanes), jnp.float32),
            pltpu.VMEM((3, rows, lanes), jnp.float32),
            pltpu.VMEM(migrant_state.shape, jnp.float32),
            pltpu.VMEM(migrant_state.shape, jnp.float32),
            dma((2, nx, halves)),
            dma((2, nx, halves)),
            dma((SUBSTEPS, 2, halves)),
            dma((SUBSTEPS, 2, halves)),
            dma((SUBSTEPS, 2, nx)),
            dma((SUBSTEPS, 2, nx)),
            dma((SUBSTEPS, 2)),
            dma((SUBSTEPS, 2)),
            dma((2,)),
            dma((2,)),
            dma((8,)),
            dma((8,)),
            dma((8,)),
            dma((8,)),
        ],
        compiler_params=pltpu.CompilerParams(
            collective_id=0, has_side_effects=True, vmem_limit_bytes=GRANT
        ),
        name="tumour_step",
    )(*inputs)
    results = (result, moved, arrived)
    result, moved, arrived = pl.pallas_call(
        deliver,
        out_shape=tuple(jax.ShapeDtypeStruct(value.shape, value.dtype) for value in results),
        in_specs=[pl.BlockSpec(memory_space=pl.ANY)] * 3,
        out_specs=(hbm, hbm, hbm),
        scratch_shapes=[dma((PIECES + 2,))],
        compiler_params=pltpu.CompilerParams(vmem_limit_bytes=GRANT),
        name="deliver",
    )(*results)
    return result, moved, jnp.transpose(arrived, (1, 0, 2))


def deliver(field_ref, disp_ref, arrived_ref, field_out, disp_out, arrived_out, sems):
    share = field_ref.shape[0] // PIECES
    routes = [
        (field_ref.at[pl.ds(piece * share, share)], field_out.at[pl.ds(piece * share, share)])
        for piece in range(PIECES)
    ]
    routes += [(disp_ref, disp_out), (arrived_ref, arrived_out)]
    copies = [
        pltpu.make_async_copy(here, there, sems.at[place])
        for place, (here, there) in enumerate(routes)
    ]
    for copy in copies:
        copy.start()
    for copy in copies:
        copy.wait()


def solution(mesh):
    return jax.shard_map(
        on_device,
        mesh=mesh,
        in_specs=(
            P(None, "gx", "gy", None),
            P(),
            P(),
            P(None, "gx", "gy", None),
            P(None, "gx", "gy", None),
            P("gx", "gy", None),
            P("gx", "gy", None),
            P("gx", "gy", None),
            P(None, "gx", "gy"),
            P(None, "gx", "gy"),
        ),
        out_specs=(P(None, "gx", "gy", None), P(None, "gx", "gy", None), P(None, "gx", "gy")),
        check_vma=False,
    )
```

```python
import jax
import jax.numpy as jnp
from jax import lax
from jax.experimental import pallas as pl
from jax.experimental.pallas import tpu as pltpu
from jax.sharding import PartitionSpec as P

BIN_XY = 4
BIN_Z = 8
SLOTS = 16
SUBSTEPS = 4
CHUNK = 8
GROUPS = 9
GRANT = 56 * 1024 * 1024
PIECES = 4

time_step = 0.15
move_step = 0.1
spread_sq = 8.0
shifts = ((-1, -1), (-1, 0), (-1, 1), (0, -1), (0, 1), (1, -1), (1, 0), (1, 1))
MESH = pl.DeviceIdType.MESH


def split(value):
    high = value.astype(jnp.bfloat16)
    return high, (value - high.astype(jnp.float32)).astype(jnp.bfloat16)


def kernel(
    field_in, rates_in, mixing_in, sec_in, pos_in, stiff_in, occ_in, off_in, state_in, live_in,
    out_ref, disp_ref, arrived_ref,
    field_ref, rates_ref, mixing_ref, sec_ref, pos_ref, stiff_ref, occ_ref, off_ref, state_ref, live_ref,
    s_load,
    buf, swap_to, swap_from, face_to, face_from, edge_from, ends_to, ends_from,
    sec_to, sec_from, off_from, src, pts, nb, own, acc, payload, landing,
    s_swap, r_swap, s_face, r_face, s_edge, r_edge, s_ends, r_ends, s_sec, r_sec,
    s_pts, r_pts, s_mig, r_mig,
):
    species, nx, ny, nz = field_ref.shape
    bins_y, lanes = stiff_ref.shape[1:]
    halves = ny // CHUNK
    pairs = CHUNK // 2
    mid = nz // 2
    groups = ((0, nx - 1), tuple(range(1, nx - 1)))
    gx, gy = lax.axis_index("gx"), lax.axis_index("gy")
    n_gx, n_gy = lax.axis_size("gx"), lax.axis_size("gy")
    p = lax.rem(gx, 2)
    mate = (gx + 1 - 2 * p, gy)
    sides = (-1, 1)

    def exists(dx, dy):
        ok = None
        for coord, count, delta in ((gx, n_gx, dx), (gy, n_gy, dy)):
            if delta != 0:
                one = coord >= -delta if delta < 0 else coord < count - delta
                ok = one if ok is None else jnp.logical_and(ok, one)
        return ok

    loads = [
        pltpu.make_async_copy(there, here, s_load.at[place])
        for place, (there, here) in enumerate(
            (
                (sec_in, sec_ref),
                (occ_in, occ_ref),
                (stiff_in, stiff_ref),
                (pos_in, pos_ref),
                (off_in, off_ref),
                (field_in, field_ref),
                (state_in, state_ref),
                (live_in, live_ref),
                (rates_in, rates_ref),
                (mixing_in, mixing_ref),
            )
        )
    ]
    for load in loads:
        load.start()

    barrier = pltpu.get_barrier_semaphore()
    for dx, dy in shifts + ((-2, 0), (2, 0)):
        @pl.when(exists(dx, dy))
        def _(dx=dx, dy=dy):
            pl.semaphore_signal(barrier, inc=1, device_id=(gx + dx, gy + dy), device_id_type=MESH)

    for load in loads[:5]:
        load.wait()
    alive = occ_ref[0].astype(jnp.float32)
    weight = stiff_ref[0] * alive
    for by in range(bins_y):
        for plane in range(3):
            pts[1, by + 1, plane : plane + 1, :] = pos_ref[plane, 0, by : by + 1, :]
        pts[1, by + 1, 3:4, :] = weight[by : by + 1]
        sec_to[by] = sec_ref[:, 0, by, :] * (alive[by : by + 1] * time_step)

    column = lax.broadcasted_iota(jnp.int32, (species, nz), 1)
    kept = (column // mid) == p
    low = column < mid
    inner = column & (mid - 1)
    rim = (1 - p) * (mid - 1)

    def turned(value):
        return pltpu.roll(value, mid, 1)

    def remote(src_ref, dst_ref, send_sem, recv_sem, device):
        return pltpu.make_async_remote_copy(
            src_ref=src_ref,
            dst_ref=dst_ref,
            send_sem=send_sem,
            recv_sem=recv_sem,
            device_id=device,
            device_id_type=MESH,
        )

    def swap(way, x, half):
        rows = pl.ds(half * pairs, pairs)
        return remote(
            swap_to.at[way, x, rows], swap_from.at[way, x, rows],
            s_swap.at[way, x, half], r_swap.at[way, x, half], mate,
        )

    def face(t, side, half):
        rows = pl.ds(half * pairs, pairs)
        return remote(
            face_to.at[t, side, rows], face_from.at[t, 1 - side, rows],
            s_face.at[t, side, half], r_face.at[t, side, half], (gx + 2 * sides[side], gy),
        )

    def edge(t, side, x):
        return remote(
            buf.at[t, x, 0 if side == 0 else ny - 1], edge_from.at[t, 1 - side, x],
            s_edge.at[t, side, x], r_edge.at[t, side, x], (gx, gy + sides[side]),
        )

    def ends(t, group):
        return remote(
            ends_to.at[t, group], ends_from.at[t, group],
            s_ends.at[t, group], r_ends.at[t, group], mate,
        )

    def secreted():
        width = lanes // 2
        return remote(
            sec_to.at[:, :, pl.ds(pl.multiple_of((1 - p) * width, width), width)],
            sec_from.at[:, :, pl.ds(pl.multiple_of(p * width, width), width)],
            s_sec.at[0], r_sec.at[0], mate,
        )

    def placed():
        return remote(off_ref, off_from, s_sec.at[1], r_sec.at[1], mate)

    def agents(index):
        dx, dy = shifts[index]
        if dy == 0:
            mine, theirs = pl.ds(1, bins_y), pl.ds(1, bins_y)
        elif dy > 0:
            mine, theirs = pl.ds(bins_y, 1), pl.ds(0, 1)
        else:
            mine, theirs = pl.ds(1, 1), pl.ds(bins_y + 1, 1)
        return remote(
            pts.at[1, mine], pts.at[1 - dx, theirs],
            s_pts.at[index], r_pts.at[index], (gx + dx, gy + dy),
        )

    def migrants(index):
        dx, dy = shifts[index]
        return remote(
            payload.at[index], landing.at[index],
            s_mig.at[index], r_mig.at[index], (gx + dx, gy + dy),
        )

    def send(copy, dx, dy):
        @pl.when(exists(dx, dy))
        def _():
            copy.start()

    def landed(copy, dx, dy):
        @pl.when(exists(-dx, -dy))
        def _():
            copy.wait_recv()

    def sent(copy, dx, dy):
        @pl.when(exists(dx, dy))
        def _():
            copy.wait_send()

    def leave(way, x, half, cells):
        for j in range(half * pairs, (half + 1) * pairs):
            swap_to[way, x, j] = jnp.where(kept, turned(cells(2 * j)), cells(2 * j + 1))
        swap(way, x, half).start()

    def enter(way, x, half, cells, keep_in):
        swap(way, x, half).wait_recv()
        for j in range(half * pairs, (half + 1) * pairs):
            came = swap_from[way, x, j]
            keep_in(2 * j, jnp.where(kept, cells(2 * j), came))
            keep_in(2 * j + 1, jnp.where(kept, cells(2 * j + 1), turned(came)))

    across = 1 + (gx > 0).astype(jnp.int32) + (gx < n_gx - 1).astype(jnp.int32)
    along = 1 + (gy > 0).astype(jnp.int32) + (gy < n_gy - 1).astype(jnp.int32)
    beyond = (gx > 1).astype(jnp.int32) + (gx < n_gx - 2).astype(jnp.int32)
    pl.semaphore_wait(barrier, across * along - 1 + beyond)

    secreted().start()
    placed().start()
    for load in loads[5:]:
        load.wait()
    order = [(x, half) for group in groups for half in range(halves) for x in group]
    for x, half in order:
        leave(0, x, half, lambda y, x=x: field_ref[:, x, y, :])
    for index in range(8):
        payload[index] = state_ref[:, index, :] * live_ref[index].astype(jnp.float32)

    for side in range(2):
        @pl.when(jnp.logical_not(exists(2 * sides[side], 0)))
        def _(side=side):
            def fill(row, carry):
                for t in range(SUBSTEPS):
                    face_from[t, side, row] = jnp.zeros((species, nz), jnp.float32)
                return carry
            lax.fori_loop(0, ny // 2, fill, 0)

        @pl.when(jnp.logical_not(exists(0, sides[side])))
        def _(side=side):
            for t in range(SUBSTEPS):
                edge_from[t, side] = jnp.zeros((nx, species, nz), jnp.float32)

    for index in range(8):
        dx, dy = shifts[index]

        @pl.when(jnp.logical_not(exists(-dx, -dy)))
        def _(index=index, dx=dx, dy=dy):
            landing[index] = jnp.zeros(landing.shape[1:], jnp.float32)
            rows = pl.ds(1, bins_y) if dy == 0 else pl.ds(0 if dy > 0 else bins_y + 1, 1)
            count = bins_y if dy == 0 else 1
            pts[1 - dx, rows] = jnp.zeros((count,) + pts.shape[2:], jnp.float32)

    secreted().wait_recv()
    placed().wait_recv()
    depth = lax.broadcasted_iota(jnp.int32, (nz, lanes), 0)
    slot = lax.broadcasted_iota(jnp.int32, (1, lanes), 1)
    layer = slot // SLOTS
    ours = (slot // (lanes // 2)) == p
    for by in range(bins_y):
        place = jnp.where(ours, off_ref[0, by : by + 1, :], pltpu.roll(off_from[0, by : by + 1, :], lanes // 2, 1))
        wide = lax.broadcasted_iota(jnp.int32, (species, lanes), 1)
        amount = jnp.where((wide // (lanes // 2)) == p, sec_to[by], sec_from[by])
        amount = jnp.concatenate(split(amount), axis=0)
        cell = jnp.where(depth == layer * BIN_Z + (place & (BIN_Z - 1)), place >> 3, -1)

        def deposit(ox, carry, by=by, amount=amount, cell=cell):
            hits = jnp.concatenate(
                [
                    jnp.where(cell == ox * BIN_XY + oy, 1.0, 0.0).astype(jnp.bfloat16)
                    for oy in range(BIN_XY)
                ],
                axis=0,
            )
            total = lax.dot_general(
                amount, hits, (((1,), (1,)), ((), ())), preferred_element_type=jnp.float32
            )
            total = total[:species] + total[species:]
            for oy in range(BIN_XY):
                src[ox, by * BIN_XY + oy] = total[:, oy * nz : (oy + 1) * nz]
            return carry

        lax.fori_loop(0, BIN_XY, deposit, 0)

    mix_high, mix_low = split(mixing_ref[...] * time_step)
    mix = jnp.concatenate([mix_high, mix_high, mix_low], axis=1)
    diagonal = lax.broadcasted_iota(jnp.int32, (species, species), 0) == lax.broadcasted_iota(
        jnp.int32, (species, species), 1
    )
    reach = jnp.sum(jnp.where(diagonal, rates_ref[...], 0.0), axis=1, keepdims=True) * time_step
    keep = 1.0 - 6.0 * reach
    reach = jnp.broadcast_to(reach, (species, nz))
    keep = jnp.broadcast_to(keep, (species, nz))

    def gather_agents():
        for index in range(8):
            landed(agents(index), *shifts[index])
        for group in range(GROUPS):
            dx, dy = group // 3, group % 3
            for by in range(bins_y):
                row = group * bins_y + by
                for plane in range(4):
                    nb[plane, row : row + 1, :] = pts[dx, by + dy, plane : plane + 1, :]
                for plane in range(3):
                    own[plane, row : row + 1, :] = pts[1, by + 1, plane : plane + 1, :]
        used = GROUPS * bins_y
        if nb.shape[1] > used:
            for plane in range(4):
                nb[plane, used:, :] = jnp.zeros((nb.shape[1] - used, lanes), jnp.float32)
            for plane in range(3):
                own[plane, used:, :] = jnp.zeros((nb.shape[1] - used, lanes), jnp.float32)
        acc[...] = jnp.zeros(acc.shape, jnp.float32)

    span = 2 * SLOTS - 1

    def forces(first, last):
        def pair(d, carry):
            other = slot + d
            near = jnp.abs((other >> 4) - (slot >> 4)) <= 1
            near = jnp.logical_and(near, jnp.logical_and(other >= 0, other < lanes))
            turn = lax.rem(lanes - d, lanes)
            apart = [own[plane] - pltpu.roll(nb[plane], turn, 1) for plane in range(3)]
            heavy = jnp.where(near, pltpu.roll(nb[3], turn, 1), 0.0)
            square = apart[0] * apart[0] + apart[1] * apart[1] + apart[2] * apart[2]
            strength = heavy * jnp.exp(square * (-1.0 / spread_sq))
            for plane in range(3):
                acc[plane] += apart[plane] * strength
            return carry

        lax.fori_loop(first, last, pair, 0)

    def row_of(x, y):
        return (x if x in groups[1] else (1 if x == 0 else 2)) * ny - ny + y

    def show(t, x, half):
        side = 0 if x == 0 else 1
        for j in range(half * pairs, (half + 1) * pairs):
            even, odd = buf[t, x, 2 * j], buf[t, x, 2 * j + 1]
            if side == 0:
                face_to[t, side, j] = jnp.where(low, even, turned(odd))
            else:
                face_to[t, side, j] = jnp.where(low, turned(even), odd)
        send(face(t, side, half), 2 * sides[side], 0)

    def finish(t, group):
        for x in groups[group]:
            for side in range(2):
                send(edge(t, side, x), 0, sides[side])
        packed = jnp.zeros((species, nz), jnp.float32)
        for x in groups[group]:
            for y in range(ny):
                row = row_of(x, y)
                moved = pltpu.roll(buf[t, x, y], lax.rem(row + nz - rim, nz), 1)
                packed = jnp.where(inner == row, moved, packed)
        ends_to[t, group] = packed
        ends(t, group).start()

    def block(t, x, half):
        first = half * CHUNK
        cells = jnp.concatenate([buf[t, x, first + k] for k in range(CHUNK)], axis=1)
        high, less = split(cells)
        mixed = jnp.dot(
            mix, jnp.concatenate([high, less, high], axis=0), preferred_element_type=jnp.float32
        )
        beyond_z = ends_from[t, 0 if x in groups[0] else 1]
        for k in range(CHUNK):
            y = first + k
            here = buf[t, x, y]
            if x > 0:
                beside = buf[t, x - 1, y]
            elif y % 2 == 0:
                beside = jnp.where(low, face_from[t, 0, y // 2], turned(buf[t, nx - 1, y]))
            else:
                beside = turned(jnp.where(low, buf[t, nx - 1, y], face_from[t, 0, y // 2]))
            if x < nx - 1:
                beside = beside + buf[t, x + 1, y]
            elif y % 2 == 0:
                beside = beside + turned(jnp.where(low, face_from[t, 1, y // 2], buf[t, 0, y]))
            else:
                beside = beside + jnp.where(low, turned(buf[t, 0, y]), face_from[t, 1, y // 2])
            beside = beside + (edge_from[t, 0, x] if y == 0 else buf[t, x, y - 1])
            beside = beside + (edge_from[t, 1, x] if y == ny - 1 else buf[t, x, y + 1])
            beside = beside + jnp.where(inner == 0, 0.0, pltpu.roll(here, 1, 1))
            beside = beside + jnp.where(inner == mid - 1, 0.0, pltpu.roll(here, nz - 1, 1))
            arriving = pltpu.roll(beyond_z, lax.rem(rim + nz - row_of(x, y), nz), 1)
            beside = beside + jnp.where(inner == rim, arriving, 0.0)
            buf[t + 1, x, y] = (
                keep * here + reach * beside + mixed[:, k * nz : (k + 1) * nz] + src[x, y]
            )

    def hold(t, x):
        def put(y, value):
            buf[t, x, y] = value
        return put

    for number, group in enumerate(groups):
        for half in range(halves):
            for x in group:
                enter(0, x, half, lambda y, x=x: field_ref[:, x, y, :], hold(0, x))
                if number == 0:
                    show(0, x, half)
        finish(0, number)
    for index in range(8):
        send(agents(index), *shifts[index])
    for index in range(8):
        send(migrants(index), *shifts[index])

    def substep(t, carry):
        for number, group in enumerate(groups):
            for x in group:
                for side in range(2):
                    landed(edge(t, side, x), 0, sides[side])
            ends(t, number).wait_recv()
            for half in range(halves):
                for x in group:
                    if number == 0:
                        side = 1 if x == 0 else 0
                        landed(face(t, side, half), 2 * sides[side], 0)
                    block(t, x, half)

                    @pl.when(t == SUBSTEPS - 1)
                    def _(x=x, half=half):
                        leave(1, x, half, lambda y, x=x: buf[SUBSTEPS, x, y])

                    if number == 0:
                        @pl.when(t < SUBSTEPS - 1)
                        def _(x=x, half=half):
                            show(t + 1, x, half)

            @pl.when(t < SUBSTEPS - 1)
            def _(number=number):
                finish(t + 1, number)

        return carry

    lax.fori_loop(0, SUBSTEPS, substep, 0)

    gather_agents()
    forces(-span, 0)
    forces(0, span + 1)
    scale = move_step * alive
    for plane in range(3):
        force = acc[plane, 0:bins_y, :]
        for group in range(1, GROUPS):
            force = force + acc[plane, group * bins_y : (group + 1) * bins_y, :]
        disp_ref[plane, 0] = scale * force

    for index in range(8):
        landed(migrants(index), *shifts[index])
        arrived_ref[:, index, :] = landing[index]
    secreted().wait_send()
    placed().wait_send()
    for index in range(8):
        sent(agents(index), *shifts[index])
        sent(migrants(index), *shifts[index])
    for x, half in order:
        swap(0, x, half).wait_send()

    def drain(t, carry):
        for side in range(2):
            for half in range(halves):
                sent(face(t, side, half), 2 * sides[side], 0)
            for x in range(nx):
                sent(edge(t, side, x), 0, sides[side])
        for number in range(2):
            ends(t, number).wait_send()
        return carry

    lax.fori_loop(0, SUBSTEPS, drain, 0)

    for x, half in order:
        def put(y, value, x=x):
            out_ref[:, x, y, :] = value

        enter(1, x, half, lambda y, x=x: buf[SUBSTEPS, x, y], put)
    for x, half in order:
        swap(1, x, half).wait_send()


def on_device(
    field, rates, mixing, secretion, positions, stiffness, occupancy, offsets, migrant_state, migrant_live
):
    species, nx, ny, nz = field.shape
    bins_y, lanes = stiffness.shape[1:]
    halves = ny // CHUNK
    kinds, state, slots = migrant_state.shape
    rows = -(-GROUPS * bins_y // 8) * 8
    vmem = pl.BlockSpec(memory_space=pltpu.VMEM)
    hbm = pl.BlockSpec(memory_space=pltpu.HBM)
    inputs = (
        field,
        rates[None],
        mixing,
        secretion,
        positions,
        stiffness,
        occupancy,
        offsets,
        jnp.transpose(migrant_state, (1, 0, 2)),
        migrant_live,
    )
    dma = pltpu.SemaphoreType.DMA
    result, moved, arrived = pl.pallas_call(
        kernel,
        out_shape=(
            jax.ShapeDtypeStruct(field.shape, jnp.float32),
            jax.ShapeDtypeStruct(positions.shape, jnp.float32),
            jax.ShapeDtypeStruct((state, kinds, slots), jnp.float32),
        ),
        in_specs=[hbm] * 10,
        out_specs=(vmem, vmem, vmem),
        scratch_shapes=[pltpu.VMEM(value.shape, value.dtype) for value in inputs]
        + [
            dma((10,)),
            pltpu.VMEM((SUBSTEPS + 1, nx, ny, species, nz), jnp.float32),
            pltpu.VMEM((2, nx, ny // 2, species, nz), jnp.float32),
            pltpu.VMEM((2, nx, ny // 2, species, nz), jnp.float32),
            pltpu.VMEM((SUBSTEPS, 2, ny // 2, species, nz), jnp.float32),
            pltpu.VMEM((SUBSTEPS, 2, ny // 2, species, nz), jnp.float32),
            pltpu.VMEM((SUBSTEPS, 2, nx, species, nz), jnp.float32),
            pltpu.VMEM((SUBSTEPS, 2, species, nz), jnp.float32),
            pltpu.VMEM((SUBSTEPS, 2, species, nz), jnp.float32),
            pltpu.VMEM((bins_y, species, lanes), jnp.float32),
            pltpu.VMEM((bins_y, species, lanes), jnp.float32),
            pltpu.VMEM(offsets.shape, jnp.int32),
            pltpu.VMEM((nx, ny, species, nz), jnp.float32),
            pltpu.VMEM((3, bins_y + 2, 8, lanes), jnp.float32),
            pltpu.VMEM((4, rows, lanes), jnp.float32),
            pltpu.VMEM((3, rows, lanes), jnp.float32),
            pltpu.VMEM((3, rows, lanes), jnp.float32),
            pltpu.VMEM(migrant_state.shape, jnp.float32),
            pltpu.VMEM(migrant_state.shape, jnp.float32),
            dma((2, nx, halves)),
            dma((2, nx, halves)),
            dma((SUBSTEPS, 2, halves)),
            dma((SUBSTEPS, 2, halves)),
            dma((SUBSTEPS, 2, nx)),
            dma((SUBSTEPS, 2, nx)),
            dma((SUBSTEPS, 2)),
            dma((SUBSTEPS, 2)),
            dma((2,)),
            dma((2,)),
            dma((8,)),
            dma((8,)),
            dma((8,)),
            dma((8,)),
        ],
        compiler_params=pltpu.CompilerParams(
            collective_id=0, has_side_effects=True, vmem_limit_bytes=GRANT
        ),
        name="tumour_step",
    )(*inputs)
    results = (result, moved, arrived)
    result, moved, arrived = pl.pallas_call(
        deliver,
        out_shape=tuple(jax.ShapeDtypeStruct(value.shape, value.dtype) for value in results),
        in_specs=[pl.BlockSpec(memory_space=pl.ANY)] * 3,
        out_specs=(hbm, hbm, hbm),
        scratch_shapes=[pltpu.VMEM(value.shape, value.dtype) for value in results]
        + [dma((PIECES + 2,)), dma((PIECES + 2,))],
        compiler_params=pltpu.CompilerParams(vmem_limit_bytes=GRANT),
        name="deliver",
    )(*results)
    return result, moved, jnp.transpose(arrived, (1, 0, 2))


def deliver(
    field_ref, disp_ref, arrived_ref, field_out, disp_out, arrived_out,
    field_held, disp_held, arrived_held, s_in, s_out,
):
    share = field_ref.shape[0] // PIECES
    routes = [
        tuple(ref.at[pl.ds(piece * share, share)] for ref in (field_ref, field_held, field_out))
        for piece in range(PIECES)
    ]
    routes += [(disp_ref, disp_held, disp_out), (arrived_ref, arrived_held, arrived_out)]
    ins = [
        pltpu.make_async_copy(here, held, s_in.at[place])
        for place, (here, held, there) in enumerate(routes)
    ]
    outs = [
        pltpu.make_async_copy(held, there, s_out.at[place])
        for place, (here, held, there) in enumerate(routes)
    ]
    for copy in ins:
        copy.start()
    for copy, onward in zip(ins, outs):
        copy.wait()
        onward.start()
    for copy in outs:
        copy.wait()


def solution(mesh):
    return jax.shard_map(
        on_device,
        mesh=mesh,
        in_specs=(
            P(None, "gx", "gy", None),
            P(),
            P(),
            P(None, "gx", "gy", None),
            P(None, "gx", "gy", None),
            P("gx", "gy", None),
            P("gx", "gy", None),
            P("gx", "gy", None),
            P(None, "gx", "gy"),
            P(None, "gx", "gy"),
        ),
        out_specs=(P(None, "gx", "gy", None), P(None, "gx", "gy", None), P(None, "gx", "gy")),
        check_vma=False,
    )
```

```python
import jax
import jax.numpy as jnp
from jax import lax
from jax.experimental import pallas as pl
from jax.experimental.pallas import tpu as pltpu
from jax.sharding import PartitionSpec as P

BIN_XY = 4
BIN_Z = 8
SLOTS = 16
SUBSTEPS = 4
CHUNK = 8
GROUPS = 9
GRANT = 56 * 1024 * 1024
PIECES = 4

time_step = 0.15
move_step = 0.1
spread_sq = 8.0
shifts = ((-1, -1), (-1, 0), (-1, 1), (0, -1), (0, 1), (1, -1), (1, 0), (1, 1))
MESH = pl.DeviceIdType.MESH


def split(value):
    high = value.astype(jnp.bfloat16)
    return high, (value - high.astype(jnp.float32)).astype(jnp.bfloat16)


def kernel(
    field_in, rates_in, mixing_in, sec_in, pos_in, stiff_in, occ_in, off_in, state_in, live_in,
    field_out, disp_out, arrived_out,
    field_ref, rates_ref, mixing_ref, sec_ref, pos_ref, stiff_ref, occ_ref, off_ref, state_ref, live_ref,
    out_ref, disp_ref, arrived_ref,
    s_load, s_store, s_block,
    buf, swap_to, swap_from, face_to, face_from, edge_from, ends_to, ends_from,
    sec_to, sec_from, off_from, src, pts, nb, own, acc, payload, landing,
    s_swap, r_swap, s_face, r_face, s_edge, r_edge, s_ends, r_ends, s_sec, r_sec,
    s_pts, r_pts, s_mig, r_mig,
):
    species, nx, ny, nz = field_ref.shape
    bins_y, lanes = stiff_ref.shape[1:]
    halves = ny // CHUNK
    pairs = CHUNK // 2
    mid = nz // 2
    groups = ((0, nx - 1), tuple(range(1, nx - 1)))
    gx, gy = lax.axis_index("gx"), lax.axis_index("gy")
    n_gx, n_gy = lax.axis_size("gx"), lax.axis_size("gy")
    p = lax.rem(gx, 2)
    mate = (gx + 1 - 2 * p, gy)
    sides = (-1, 1)

    def exists(dx, dy):
        ok = None
        for coord, count, delta in ((gx, n_gx, dx), (gy, n_gy, dy)):
            if delta != 0:
                one = coord >= -delta if delta < 0 else coord < count - delta
                ok = one if ok is None else jnp.logical_and(ok, one)
        return ok

    loads = [
        pltpu.make_async_copy(there, here, s_load.at[place])
        for place, (there, here) in enumerate(
            (
                (sec_in, sec_ref),
                (occ_in, occ_ref),
                (stiff_in, stiff_ref),
                (pos_in, pos_ref),
                (off_in, off_ref),
                (field_in, field_ref),
                (state_in, state_ref),
                (live_in, live_ref),
                (rates_in, rates_ref),
                (mixing_in, mixing_ref),
            )
        )
    ]
    for load in loads:
        load.start()

    barrier = pltpu.get_barrier_semaphore()
    for dx, dy in shifts + ((-2, 0), (2, 0)):
        @pl.when(exists(dx, dy))
        def _(dx=dx, dy=dy):
            pl.semaphore_signal(barrier, inc=1, device_id=(gx + dx, gy + dy), device_id_type=MESH)

    for load in loads[:5]:
        load.wait()
    alive = occ_ref[0].astype(jnp.float32)
    weight = stiff_ref[0] * alive
    for by in range(bins_y):
        for plane in range(3):
            pts[1, by + 1, plane : plane + 1, :] = pos_ref[plane, 0, by : by + 1, :]
        pts[1, by + 1, 3:4, :] = weight[by : by + 1]
        sec_to[by] = sec_ref[:, 0, by, :] * (alive[by : by + 1] * time_step)

    column = lax.broadcasted_iota(jnp.int32, (species, nz), 1)
    kept = (column // mid) == p
    low = column < mid
    inner = column & (mid - 1)
    rim = (1 - p) * (mid - 1)

    def turned(value):
        return pltpu.roll(value, mid, 1)

    def remote(src_ref, dst_ref, send_sem, recv_sem, device):
        return pltpu.make_async_remote_copy(
            src_ref=src_ref,
            dst_ref=dst_ref,
            send_sem=send_sem,
            recv_sem=recv_sem,
            device_id=device,
            device_id_type=MESH,
        )

    def swap(way, x, half):
        rows = pl.ds(half * pairs, pairs)
        return remote(
            swap_to.at[way, x, rows], swap_from.at[way, x, rows],
            s_swap.at[way, x, half], r_swap.at[way, x, half], mate,
        )

    def face(t, side, half):
        rows = pl.ds(half * pairs, pairs)
        return remote(
            face_to.at[t, side, rows], face_from.at[t, 1 - side, rows],
            s_face.at[t, side, half], r_face.at[t, side, half], (gx + 2 * sides[side], gy),
        )

    def edge(t, side, x):
        return remote(
            buf.at[t, x, 0 if side == 0 else ny - 1], edge_from.at[t, 1 - side, x],
            s_edge.at[t, side, x], r_edge.at[t, side, x], (gx, gy + sides[side]),
        )

    def ends(t, group):
        return remote(
            ends_to.at[t, group], ends_from.at[t, group],
            s_ends.at[t, group], r_ends.at[t, group], mate,
        )

    def secreted():
        width = lanes // 2
        return remote(
            sec_to.at[:, :, pl.ds(pl.multiple_of((1 - p) * width, width), width)],
            sec_from.at[:, :, pl.ds(pl.multiple_of(p * width, width), width)],
            s_sec.at[0], r_sec.at[0], mate,
        )

    def placed():
        return remote(off_ref, off_from, s_sec.at[1], r_sec.at[1], mate)

    def agents(index):
        dx, dy = shifts[index]
        if dy == 0:
            mine, theirs = pl.ds(1, bins_y), pl.ds(1, bins_y)
        elif dy > 0:
            mine, theirs = pl.ds(bins_y, 1), pl.ds(0, 1)
        else:
            mine, theirs = pl.ds(1, 1), pl.ds(bins_y + 1, 1)
        return remote(
            pts.at[1, mine], pts.at[1 - dx, theirs],
            s_pts.at[index], r_pts.at[index], (gx + dx, gy + dy),
        )

    def migrants(index):
        dx, dy = shifts[index]
        return remote(
            payload.at[index], landing.at[index],
            s_mig.at[index], r_mig.at[index], (gx + dx, gy + dy),
        )

    def send(copy, dx, dy):
        @pl.when(exists(dx, dy))
        def _():
            copy.start()

    def landed(copy, dx, dy):
        @pl.when(exists(-dx, -dy))
        def _():
            copy.wait_recv()

    def sent(copy, dx, dy):
        @pl.when(exists(dx, dy))
        def _():
            copy.wait_send()

    def leave(way, x, half, cells):
        for j in range(half * pairs, (half + 1) * pairs):
            swap_to[way, x, j] = jnp.where(kept, turned(cells(2 * j)), cells(2 * j + 1))
        swap(way, x, half).start()

    def enter(way, x, half, cells, keep_in):
        swap(way, x, half).wait_recv()
        for j in range(half * pairs, (half + 1) * pairs):
            came = swap_from[way, x, j]
            keep_in(2 * j, jnp.where(kept, cells(2 * j), came))
            keep_in(2 * j + 1, jnp.where(kept, cells(2 * j + 1), turned(came)))

    across = 1 + (gx > 0).astype(jnp.int32) + (gx < n_gx - 1).astype(jnp.int32)
    along = 1 + (gy > 0).astype(jnp.int32) + (gy < n_gy - 1).astype(jnp.int32)
    beyond = (gx > 1).astype(jnp.int32) + (gx < n_gx - 2).astype(jnp.int32)
    pl.semaphore_wait(barrier, across * along - 1 + beyond)

    secreted().start()
    placed().start()
    for load in loads[5:]:
        load.wait()
    order = [(x, half) for group in groups for half in range(halves) for x in group]
    for x, half in order:
        leave(0, x, half, lambda y, x=x: field_ref[:, x, y, :])
    for index in range(8):
        payload[index] = state_ref[:, index, :] * live_ref[index].astype(jnp.float32)

    for side in range(2):
        @pl.when(jnp.logical_not(exists(2 * sides[side], 0)))
        def _(side=side):
            def fill(row, carry):
                for t in range(SUBSTEPS):
                    face_from[t, side, row] = jnp.zeros((species, nz), jnp.float32)
                return carry
            lax.fori_loop(0, ny // 2, fill, 0)

        @pl.when(jnp.logical_not(exists(0, sides[side])))
        def _(side=side):
            for t in range(SUBSTEPS):
                edge_from[t, side] = jnp.zeros((nx, species, nz), jnp.float32)

    for index in range(8):
        dx, dy = shifts[index]

        @pl.when(jnp.logical_not(exists(-dx, -dy)))
        def _(index=index, dx=dx, dy=dy):
            landing[index] = jnp.zeros(landing.shape[1:], jnp.float32)
            rows = pl.ds(1, bins_y) if dy == 0 else pl.ds(0 if dy > 0 else bins_y + 1, 1)
            count = bins_y if dy == 0 else 1
            pts[1 - dx, rows] = jnp.zeros((count,) + pts.shape[2:], jnp.float32)

    secreted().wait_recv()
    placed().wait_recv()
    depth = lax.broadcasted_iota(jnp.int32, (nz, lanes), 0)
    slot = lax.broadcasted_iota(jnp.int32, (1, lanes), 1)
    layer = slot // SLOTS
    ours = (slot // (lanes // 2)) == p
    for by in range(bins_y):
        place = jnp.where(ours, off_ref[0, by : by + 1, :], pltpu.roll(off_from[0, by : by + 1, :], lanes // 2, 1))
        wide = lax.broadcasted_iota(jnp.int32, (species, lanes), 1)
        amount = jnp.where((wide // (lanes // 2)) == p, sec_to[by], sec_from[by])
        amount = jnp.concatenate(split(amount), axis=0)
        cell = jnp.where(depth == layer * BIN_Z + (place & (BIN_Z - 1)), place >> 3, -1)

        def deposit(ox, carry, by=by, amount=amount, cell=cell):
            hits = jnp.concatenate(
                [
                    jnp.where(cell == ox * BIN_XY + oy, 1.0, 0.0).astype(jnp.bfloat16)
                    for oy in range(BIN_XY)
                ],
                axis=0,
            )
            total = lax.dot_general(
                amount, hits, (((1,), (1,)), ((), ())), preferred_element_type=jnp.float32
            )
            total = total[:species] + total[species:]
            for oy in range(BIN_XY):
                src[ox, by * BIN_XY + oy] = total[:, oy * nz : (oy + 1) * nz]
            return carry

        lax.fori_loop(0, BIN_XY, deposit, 0)

    mix_high, mix_low = split(mixing_ref[...] * time_step)
    mix = jnp.concatenate([mix_high, mix_high, mix_low], axis=1)
    diagonal = lax.broadcasted_iota(jnp.int32, (species, species), 0) == lax.broadcasted_iota(
        jnp.int32, (species, species), 1
    )
    reach = jnp.sum(jnp.where(diagonal, rates_ref[...], 0.0), axis=1, keepdims=True) * time_step
    keep = 1.0 - 6.0 * reach
    reach = jnp.broadcast_to(reach, (species, nz))
    keep = jnp.broadcast_to(keep, (species, nz))

    def gather_agents():
        for index in range(8):
            landed(agents(index), *shifts[index])
        for group in range(GROUPS):
            dx, dy = group // 3, group % 3
            for by in range(bins_y):
                row = group * bins_y + by
                for plane in range(4):
                    nb[plane, row : row + 1, :] = pts[dx, by + dy, plane : plane + 1, :]
                for plane in range(3):
                    own[plane, row : row + 1, :] = pts[1, by + 1, plane : plane + 1, :]
        used = GROUPS * bins_y
        if nb.shape[1] > used:
            for plane in range(4):
                nb[plane, used:, :] = jnp.zeros((nb.shape[1] - used, lanes), jnp.float32)
            for plane in range(3):
                own[plane, used:, :] = jnp.zeros((nb.shape[1] - used, lanes), jnp.float32)
        acc[...] = jnp.zeros(acc.shape, jnp.float32)

    span = 2 * SLOTS - 1

    def forces(first, last):
        def pair(d, carry):
            other = slot + d
            near = jnp.abs((other >> 4) - (slot >> 4)) <= 1
            near = jnp.logical_and(near, jnp.logical_and(other >= 0, other < lanes))
            turn = lax.rem(lanes - d, lanes)
            apart = [own[plane] - pltpu.roll(nb[plane], turn, 1) for plane in range(3)]
            heavy = jnp.where(near, pltpu.roll(nb[3], turn, 1), 0.0)
            square = apart[0] * apart[0] + apart[1] * apart[1] + apart[2] * apart[2]
            strength = heavy * jnp.exp(square * (-1.0 / spread_sq))
            for plane in range(3):
                acc[plane] += apart[plane] * strength
            return carry

        lax.fori_loop(first, last, pair, 0)

    def row_of(x, y):
        return (x if x in groups[1] else (1 if x == 0 else 2)) * ny - ny + y

    def show(t, x, half):
        side = 0 if x == 0 else 1
        for j in range(half * pairs, (half + 1) * pairs):
            even, odd = buf[t, x, 2 * j], buf[t, x, 2 * j + 1]
            if side == 0:
                face_to[t, side, j] = jnp.where(low, even, turned(odd))
            else:
                face_to[t, side, j] = jnp.where(low, turned(even), odd)
        send(face(t, side, half), 2 * sides[side], 0)

    def finish(t, group):
        for x in groups[group]:
            for side in range(2):
                send(edge(t, side, x), 0, sides[side])
        packed = jnp.zeros((species, nz), jnp.float32)
        for x in groups[group]:
            for y in range(ny):
                row = row_of(x, y)
                moved = pltpu.roll(buf[t, x, y], lax.rem(row + nz - rim, nz), 1)
                packed = jnp.where(inner == row, moved, packed)
        ends_to[t, group] = packed
        ends(t, group).start()

    def block(t, x, half):
        first = half * CHUNK
        cells = jnp.concatenate([buf[t, x, first + k] for k in range(CHUNK)], axis=1)
        high, less = split(cells)
        mixed = jnp.dot(
            mix, jnp.concatenate([high, less, high], axis=0), preferred_element_type=jnp.float32
        )
        beyond_z = ends_from[t, 0 if x in groups[0] else 1]
        for k in range(CHUNK):
            y = first + k
            here = buf[t, x, y]
            if x > 0:
                beside = buf[t, x - 1, y]
            elif y % 2 == 0:
                beside = jnp.where(low, face_from[t, 0, y // 2], turned(buf[t, nx - 1, y]))
            else:
                beside = turned(jnp.where(low, buf[t, nx - 1, y], face_from[t, 0, y // 2]))
            if x < nx - 1:
                beside = beside + buf[t, x + 1, y]
            elif y % 2 == 0:
                beside = beside + turned(jnp.where(low, face_from[t, 1, y // 2], buf[t, 0, y]))
            else:
                beside = beside + jnp.where(low, turned(buf[t, 0, y]), face_from[t, 1, y // 2])
            beside = beside + (edge_from[t, 0, x] if y == 0 else buf[t, x, y - 1])
            beside = beside + (edge_from[t, 1, x] if y == ny - 1 else buf[t, x, y + 1])
            beside = beside + jnp.where(inner == 0, 0.0, pltpu.roll(here, 1, 1))
            beside = beside + jnp.where(inner == mid - 1, 0.0, pltpu.roll(here, nz - 1, 1))
            arriving = pltpu.roll(beyond_z, lax.rem(rim + nz - row_of(x, y), nz), 1)
            beside = beside + jnp.where(inner == rim, arriving, 0.0)
            buf[t + 1, x, y] = (
                keep * here + reach * beside + mixed[:, k * nz : (k + 1) * nz] + src[x, y]
            )

    def hold(t, x):
        def put(y, value):
            buf[t, x, y] = value
        return put

    for number, group in enumerate(groups):
        for half in range(halves):
            for x in group:
                enter(0, x, half, lambda y, x=x: field_ref[:, x, y, :], hold(0, x))
                if number == 0:
                    show(0, x, half)
        finish(0, number)

    def substep(t, carry):
        for number, group in enumerate(groups):
            for x in group:
                for side in range(2):
                    landed(edge(t, side, x), 0, sides[side])
            ends(t, number).wait_recv()
            for half in range(halves):
                for x in group:
                    if number == 0:
                        side = 1 if x == 0 else 0
                        landed(face(t, side, half), 2 * sides[side], 0)
                    block(t, x, half)

                    @pl.when(t == SUBSTEPS - 1)
                    def _(x=x, half=half):
                        leave(1, x, half, lambda y, x=x: buf[SUBSTEPS, x, y])

                    if number == 0:
                        @pl.when(t < SUBSTEPS - 1)
                        def _(x=x, half=half):
                            show(t + 1, x, half)

            @pl.when(t < SUBSTEPS - 1)
            def _(number=number):
                finish(t + 1, number)

        @pl.when(t == 0)
        def _():
            for index in range(8):
                send(agents(index), *shifts[index])

        for turn in (1, 2):
            @pl.when(t == turn)
            def _(turn=turn):
                for index in range(4 * turn - 4, 4 * turn):
                    send(migrants(index), *shifts[index])

        return carry

    lax.fori_loop(0, SUBSTEPS, substep, 0)

    gather_agents()
    forces(-span, 0)
    forces(0, span + 1)
    scale = move_step * alive
    for plane in range(3):
        force = acc[plane, 0:bins_y, :]
        for group in range(1, GROUPS):
            force = force + acc[plane, group * bins_y : (group + 1) * bins_y, :]
        disp_ref[plane, 0] = scale * force

    for index in range(8):
        landed(migrants(index), *shifts[index])
        arrived_ref[:, index, :] = landing[index]
    stores = [
        pltpu.make_async_copy(disp_ref, disp_out, s_store.at[0]),
        pltpu.make_async_copy(arrived_ref, arrived_out, s_store.at[1]),
    ]
    for store in stores:
        store.start()
    secreted().wait_send()
    placed().wait_send()
    for index in range(8):
        sent(agents(index), *shifts[index])
        sent(migrants(index), *shifts[index])
    for x, half in order:
        swap(0, x, half).wait_send()

    def drain(t, carry):
        for side in range(2):
            for half in range(halves):
                sent(face(t, side, half), 2 * sides[side], 0)
            for x in range(nx):
                sent(edge(t, side, x), 0, sides[side])
        for number in range(2):
            ends(t, number).wait_send()
        return carry

    lax.fori_loop(0, SUBSTEPS, drain, 0)

    for x, half in order:
        def put(y, value, x=x):
            out_ref[:, x, y, :] = value

        enter(1, x, half, lambda y, x=x: buf[SUBSTEPS, x, y], put)
        rows = pl.ds(half * CHUNK, CHUNK)
        store = pltpu.make_async_copy(
            out_ref.at[:, x, rows], field_out.at[:, x, rows], s_block.at[x, half]
        )
        store.start()
        stores.append(store)
    for x, half in order:
        swap(1, x, half).wait_send()
    for store in stores:
        store.wait()


def on_device(
    field, rates, mixing, secretion, positions, stiffness, occupancy, offsets, migrant_state, migrant_live
):
    species, nx, ny, nz = field.shape
    bins_y, lanes = stiffness.shape[1:]
    halves = ny // CHUNK
    kinds, state, slots = migrant_state.shape
    rows = -(-GROUPS * bins_y // 8) * 8
    hbm = pl.BlockSpec(memory_space=pltpu.HBM)
    inputs = (
        field,
        rates[None],
        mixing,
        secretion,
        positions,
        stiffness,
        occupancy,
        offsets,
        jnp.transpose(migrant_state, (1, 0, 2)),
        migrant_live,
    )
    dma = pltpu.SemaphoreType.DMA
    result, moved, arrived = pl.pallas_call(
        kernel,
        out_shape=(
            jax.ShapeDtypeStruct(field.shape, jnp.float32),
            jax.ShapeDtypeStruct(positions.shape, jnp.float32),
            jax.ShapeDtypeStruct((state, kinds, slots), jnp.float32),
        ),
        in_specs=[hbm] * 10,
        out_specs=(hbm, hbm, hbm),
        scratch_shapes=[pltpu.VMEM(value.shape, value.dtype) for value in inputs]
        + [
            pltpu.VMEM(field.shape, jnp.float32),
            pltpu.VMEM(positions.shape, jnp.float32),
            pltpu.VMEM((state, kinds, slots), jnp.float32),
            dma((10,)),
            dma((2,)),
            dma((nx, halves)),
            pltpu.VMEM((SUBSTEPS + 1, nx, ny, species, nz), jnp.float32),
            pltpu.VMEM((2, nx, ny // 2, species, nz), jnp.float32),
            pltpu.VMEM((2, nx, ny // 2, species, nz), jnp.float32),
            pltpu.VMEM((SUBSTEPS, 2, ny // 2, species, nz), jnp.float32),
            pltpu.VMEM((SUBSTEPS, 2, ny // 2, species, nz), jnp.float32),
            pltpu.VMEM((SUBSTEPS, 2, nx, species, nz), jnp.float32),
            pltpu.VMEM((SUBSTEPS, 2, species, nz), jnp.float32),
            pltpu.VMEM((SUBSTEPS, 2, species, nz), jnp.float32),
            pltpu.VMEM((bins_y, species, lanes), jnp.float32),
            pltpu.VMEM((bins_y, species, lanes), jnp.float32),
            pltpu.VMEM(offsets.shape, jnp.int32),
            pltpu.VMEM((nx, ny, species, nz), jnp.float32),
            pltpu.VMEM((3, bins_y + 2, 8, lanes), jnp.float32),
            pltpu.VMEM((4, rows, lanes), jnp.float32),
            pltpu.VMEM((3, rows, lanes), jnp.float32),
            pltpu.VMEM((3, rows, lanes), jnp.float32),
            pltpu.VMEM(migrant_state.shape, jnp.float32),
            pltpu.VMEM(migrant_state.shape, jnp.float32),
            dma((2, nx, halves)),
            dma((2, nx, halves)),
            dma((SUBSTEPS, 2, halves)),
            dma((SUBSTEPS, 2, halves)),
            dma((SUBSTEPS, 2, nx)),
            dma((SUBSTEPS, 2, nx)),
            dma((SUBSTEPS, 2)),
            dma((SUBSTEPS, 2)),
            dma((2,)),
            dma((2,)),
            dma((8,)),
            dma((8,)),
            dma((8,)),
            dma((8,)),
        ],
        compiler_params=pltpu.CompilerParams(
            collective_id=0, has_side_effects=True, vmem_limit_bytes=GRANT
        ),
        name="tumour_step",
    )(*inputs)
    results = (result, moved, arrived)
    result, moved, arrived = pl.pallas_call(
        deliver,
        out_shape=tuple(jax.ShapeDtypeStruct(value.shape, value.dtype) for value in results),
        in_specs=[pl.BlockSpec(memory_space=pl.ANY)] * 3,
        out_specs=(hbm, hbm, hbm),
        scratch_shapes=[pltpu.VMEM(value.shape, value.dtype) for value in results]
        + [dma((PIECES + 2,)), dma((PIECES + 2,))],
        compiler_params=pltpu.CompilerParams(vmem_limit_bytes=GRANT),
        name="deliver",
    )(*results)
    return result, moved, jnp.transpose(arrived, (1, 0, 2))


def deliver(
    field_ref, disp_ref, arrived_ref, field_out, disp_out, arrived_out,
    field_held, disp_held, arrived_held, s_in, s_out,
):
    share = field_ref.shape[0] // PIECES
    routes = [
        tuple(ref.at[pl.ds(piece * share, share)] for ref in (field_ref, field_held, field_out))
        for piece in range(PIECES)
    ]
    routes += [(disp_ref, disp_held, disp_out), (arrived_ref, arrived_held, arrived_out)]
    ins = [
        pltpu.make_async_copy(here, held, s_in.at[place])
        for place, (here, held, there) in enumerate(routes)
    ]
    outs = [
        pltpu.make_async_copy(held, there, s_out.at[place])
        for place, (here, held, there) in enumerate(routes)
    ]
    for copy in ins:
        copy.start()
    for copy, onward in zip(ins, outs):
        copy.wait()
        onward.start()
    for copy in outs:
        copy.wait()


def solution(mesh):
    return jax.shard_map(
        on_device,
        mesh=mesh,
        in_specs=(
            P(None, "gx", "gy", None),
            P(),
            P(),
            P(None, "gx", "gy", None),
            P(None, "gx", "gy", None),
            P("gx", "gy", None),
            P("gx", "gy", None),
            P("gx", "gy", None),
            P(None, "gx", "gy"),
            P(None, "gx", "gy"),
        ),
        out_specs=(P(None, "gx", "gy", None), P(None, "gx", "gy", None), P(None, "gx", "gy")),
        check_vma=False,
    )
```
